256 devices in a mesh: lat: 8 (over x_hi, y), lon: 32 (over z, x_lo, core).
Axes of the slice: x: 4 (x_hi: 2, x_lo: 2; x = x_hi * 2 + x_lo), y: 4, z: 8, core: 2. Of those that a mesh axis runs over, the one named last changes fastest.
Arguments:
- tokens: bfloat16 [4, 48, 384, 512], P(None, 'lat', 'lon'), may hold values from -6 to 6
- weights: bfloat16 [2048, 512], replicated, may hold values from -1 to 1, as said below
- out_grad: bfloat16 [4, 48, 384, 512], P(None, 'lat', 'lon'), may hold values from -6 to 6
Outputs:
- mixed: bfloat16 [4, 48, 384, 512], P(None, 'lat', 'lon')
- token_grads: bfloat16 [4, 48, 384, 512], P(None, 'lat', 'lon')
- weight_grads: float32 [2048, 512], P(('lat', 'lon'))
The draws below stay inside these ranges and needn't reach their ends.
Inputs may be any that keep to these rules, and one draw needn't show every extreme that they name: Rows 0 to 511 of weights give queries, the next 512 keys, the next 512 values, the last 512 the output projection.
All inputs are finite; a program needn't handle non-finite values.
Results may differ from the reference program's by a relative error of at most 0.0091.
Values may be sent and summed in bfloat16 or wider, within the bound.
No kernel may reach another device: no remote copies, remote signals or barrier semaphores. Data moves between devices by JAX's collectives and lax.ppermute only.
A program may use at most 128 MiB of HBM per device.

```python
import jax
import jax.numpy as jnp
from jax import lax

D = 512
HEADS = 8
LV = 4
WIN_LEV = 2
WIN_LAT = 6
WIN_LON = 12
NLAT = 48
NLON = 384


def draw_weights(key, part):
    key = jax.random.fold_in(key, 11)
    pattern_key = jax.random.fold_in(key, 0)
    pattern = jnp.clip(jax.random.normal(pattern_key, (4 * D, D), jnp.float32), -3.0, 3.0)
    return (pattern * D ** (-0.5)).astype(jnp.bfloat16)


def strengthened(drawn, rng, source, target, parts, factor):
    owner, partner = [(jnp.arange(drawn.shape[axis_at]) // (drawn.shape[axis_at] // parts)).reshape([-1 if axis == axis_at else 1 for axis in range(drawn.ndim)]) for axis_at in (source, target)]
    chosen = jax.random.permutation(rng, parts)[partner]
    strong = (owner == chosen) | (owner == (partner + parts // 2) % parts)
    return jnp.where(strong, factor * drawn, drawn)


def block_levels(own_key, extent, cuts, low, largest):
    factor_of = 1.0
    for axis_at, blocks in cuts:
        heights = jax.random.uniform(jax.random.fold_in(jax.random.fold_in(own_key, 6), axis_at), (blocks,), jnp.float32, low / len(cuts), largest / len(cuts))
        factor_of = factor_of * jnp.repeat(jnp.exp(heights), extent[axis_at] // blocks).reshape((-1,) + (1,) * (len(extent) - 1 - axis_at))
    return factor_of


def noise(rng, dims, scale, most, pieces=(), kind=jnp.bfloat16):
    loudness = block_levels(rng, dims, pieces, -0.22, 0.18) if pieces else 1.0
    result = jax.random.normal(rng, dims, jnp.float32) * scale * loudness
    return jnp.minimum(jnp.maximum(result, -most), most).astype(kind)


def bell_draw_with(key, shape, scale, limit, shards, heavy, held_as=jnp.bfloat16):
    entries = scale * jax.random.normal(key, shape, jnp.float32)
    if shards:
        entries = entries * block_levels(key, shape, shards, -0.22, 0.18)
    return jnp.clip(strengthened(entries, jax.random.fold_in(key, 3), *heavy), -limit, limit).astype(held_as)


def setup_inputs(seed: int = 0) -> dict:
    key_of = jax.random.split(jax.random.key(seed), 4)
    return {
        "tokens": noise(key_of[0], (LV, NLAT, NLON, D), 1.0, 6.0, ((1, 8), (2, 32))),
        "weights": draw_weights(jax.random.fold_in(key_of[3], 71), 0),
        "out_grad": bell_draw_with(key_of[2], (LV, NLAT, NLON, D), 1.0, 6.0, ((1, 8), (2, 32)), (2, 3, 32, 2.75)),
    }


epsilon = 1e-05
masked_score = -1e+30

def normalize(values):
    average = lax.optimization_barrier(jnp.mean(values, axis=-1, keepdims=True))
    centred = values - average
    inverse = lax.rsqrt(lax.optimization_barrier(jnp.mean(centred * centred, axis=-1, keepdims=True)) + epsilon)
    return (centred * inverse, inverse)

def product(form, left, right):
    return jnp.einsum(form, left.astype(jnp.float32), right.astype(jnp.float32))

def window_pass(query, keys, values, ctx_grad, key_valid):
    score_scale = query.shape[-1] ** (-0.5)
    scores = product('whqe,whke->whqk', query, keys) * score_scale
    scores = jnp.where(key_valid[:, None, None, :], scores, masked_score)
    peak = lax.optimization_barrier(jnp.max(scores, axis=-1, keepdims=True))
    raised = jnp.exp(scores - peak)
    probs = raised / lax.optimization_barrier(jnp.sum(raised, axis=-1, keepdims=True))
    prob_weights = probs.astype(jnp.bfloat16)
    context = product('whqk,whke->whqe', prob_weights, values).astype(jnp.bfloat16)
    prob_grad = product('whqe,whke->whqk', ctx_grad, values)
    value_grad = product('whqk,whqe->whke', prob_weights, ctx_grad)
    score_grad = (probs * (prob_grad - lax.optimization_barrier(jnp.sum(prob_grad * probs, axis=-1, keepdims=True))) * score_scale).astype(jnp.bfloat16)
    query_grad = product('whqk,whke->whqe', score_grad, keys)
    key_grad = product('whqk,whqe->whke', score_grad, query)
    return (context, query_grad, key_grad, value_grad)

def split_windows(field, head_count):
    level_num, lat_num, lon_num, feat_num = field.shape
    shaped = field.reshape(level_num // WIN_LEV, WIN_LEV, lat_num // WIN_LAT, WIN_LAT, lon_num // WIN_LON, WIN_LON, head_count, feat_num // head_count)
    shaped = shaped.transpose(2, 0, 4, 6, 1, 3, 5, 7)
    return shaped.reshape(lat_num // WIN_LAT, level_num // WIN_LEV * (lon_num // WIN_LON), head_count, WIN_LEV * WIN_LAT * WIN_LON, feat_num // head_count)

def join_windows(blocks, level_num, lat_num, lon_num):
    head_count = blocks.shape[2]
    head_size = blocks.shape[4]
    shaped = blocks.reshape(lat_num // WIN_LAT, level_num // WIN_LEV, lon_num // WIN_LON, head_count, WIN_LEV, WIN_LAT, WIN_LON, head_size)
    shaped = shaped.transpose(1, 4, 0, 5, 2, 6, 3, 7)
    return shaped.reshape(level_num, lat_num, lon_num, head_count * head_size)

def reference(tokens, weights, out_grad):
    level_num, lat_num, lon_num, feat_num = tokens.shape
    lev_pad = WIN_LEV // 2
    lat_pad = WIN_LAT // 2
    lon_shift = WIN_LON // 2
    x_float = tokens.astype(jnp.float32)
    normed_exact, inverse = normalize(x_float)
    normed = normed_exact.astype(jnp.bfloat16)
    flat_normed = normed.reshape(-1, feat_num)
    w_proj = weights[:3 * feat_num]
    w_out = weights[3 * feat_num:]
    projected = jnp.dot(flat_normed, w_proj.T, preferred_element_type=jnp.float32).astype(jnp.bfloat16)
    projected = projected.reshape(level_num, lat_num, lon_num, 3 * feat_num)
    flat_grad = out_grad.reshape(-1, feat_num)
    ctx_grad = jnp.dot(flat_grad, w_out, preferred_element_type=jnp.float32).astype(jnp.bfloat16)
    ctx_grad = ctx_grad.reshape(level_num, lat_num, lon_num, feat_num)

    def arrange(field):
        rolled = jnp.roll(field, lon_shift, axis=2)
        return jnp.pad(rolled, ((lev_pad, lev_pad), (lat_pad, lat_pad), (0, 0), (0, 0)))

    def restore(field):
        inner = field[lev_pad:lev_pad + level_num, lat_pad:lat_pad + lat_num]
        return jnp.roll(inner, -lon_shift, axis=2)
    full_levels = level_num + 2 * lev_pad
    full_lat = lat_num + 2 * lat_pad
    level_index = jnp.arange(full_levels)
    lat_index = jnp.arange(full_lat)
    level_ok = (level_index >= lev_pad) & (level_index < lev_pad + level_num)
    lat_ok = (lat_index >= lat_pad) & (lat_index < lat_pad + lat_num)
    valid = level_ok[:, None, None] & lat_ok[None, :, None] & jnp.ones((1, 1, lon_num), dtype=jnp.bool_)
    valid_windows = split_windows(valid[..., None], 1)[:, :, 0, :, 0]
    query_w = split_windows(arrange(projected[..., :feat_num]), HEADS)
    keys_w = split_windows(arrange(projected[..., feat_num:2 * feat_num]), HEADS)
    values_w = split_windows(arrange(projected[..., 2 * feat_num:]), HEADS)
    ctx_grad_w = split_windows(arrange(ctx_grad), HEADS)

    def window_step(packed):
        return window_pass(packed[0], packed[1], packed[2], packed[3], packed[4])
    context_w, query_grad_w, key_grad_w, value_grad_w = lax.map(window_step, (query_w, keys_w, values_w, ctx_grad_w, valid_windows))
    context = restore(join_windows(context_w, full_levels, full_lat, lon_num))
    query_grad = restore(join_windows(query_grad_w, full_levels, full_lat, lon_num)).astype(jnp.bfloat16)
    key_grad = restore(join_windows(key_grad_w, full_levels, full_lat, lon_num)).astype(jnp.bfloat16)
    value_grad = restore(join_windows(value_grad_w, full_levels, full_lat, lon_num)).astype(jnp.bfloat16)
    flat_context = context.reshape(-1, feat_num)
    mixed = (x_float + jnp.dot(flat_context, w_out.T, preferred_element_type=jnp.float32).reshape(tokens.shape)).astype(jnp.bfloat16)
    proj_grad = jnp.concatenate([query_grad, key_grad, value_grad], axis=-1).reshape(-1, 3 * feat_num)
    weight_grads = jnp.concatenate([jnp.dot(proj_grad.T, flat_normed, preferred_element_type=jnp.float32), jnp.dot(flat_grad.T, flat_context, preferred_element_type=jnp.float32)], axis=0)
    normed_grad = jnp.dot(proj_grad, w_proj, preferred_element_type=jnp.float32).reshape(tokens.shape)
    correction = normed_grad - lax.optimization_barrier(jnp.mean(normed_grad, axis=-1, keepdims=True)) - normed_exact * lax.optimization_barrier(jnp.mean(normed_grad * normed_exact, axis=-1, keepdims=True))
    token_grads = (out_grad.astype(jnp.float32) + inverse * correction).astype(jnp.bfloat16)
    return (mixed, token_grads, weight_grads)
```

```python
import jax
import jax.numpy as jnp
from jax import lax
from jax.experimental import pallas as pl
from jax.experimental.pallas import tpu as pltpu
from jax.sharding import Mesh, PartitionSpec as P

HEADS = 8
FEAT = 512
HEAD = 64
WIN = 144
epsilon = 1e-05
masked_score = -1e30
LAT = ("xh", "y")
LON = ("zh", "zl", "xl", "c")
ALL = LAT + LON
VMEM = pl.BlockSpec(memory_space=pltpu.VMEM)
HBM = pl.BlockSpec(memory_space=pltpu.HBM)
ANY = pl.BlockSpec(memory_space=pl.ANY)
LOG2E = 1.4426950408889634
f32 = jnp.float32
bf16 = jnp.bfloat16


def nn(a, b):
    return lax.dot_general(a, b, (((1,), (0,)), ((), ())), preferred_element_type=f32)


def nt(a, b):
    return lax.dot_general(a, b, (((1,), (1,)), ((), ())), preferred_element_type=f32)


def call(kernel, outs, scratch, mib, args, kinds=None, out_kind=VMEM):
    return pl.pallas_call(
        kernel,
        out_shape=[jax.ShapeDtypeStruct(s, d) for s, d in outs],
        in_specs=[VMEM] * len(args) if kinds is None else kinds,
        out_specs=[out_kind] * len(outs),
        scratch_shapes=scratch,
        compiler_params=pltpu.CompilerParams(vmem_limit_bytes=mib * 2**20),
    )(*args)


def normalize(x):
    mean = jnp.mean(x, axis=-1, keepdims=True)
    centred = x - mean
    inverse = lax.rsqrt(jnp.mean(centred * centred, axis=-1, keepdims=True) + epsilon)
    return centred * inverse, inverse


QUAD = (2, 3, 6, 4, FEAT)


def quadrants():
    far = 3 - 3 * lax.axis_index("c")
    near = 3 - far
    return [
        (pl.ds(lat, 3), pl.ds(lon, 6)) for lat, lon in ((far, 6), (near, 0), (near, 6), (far, 0))
    ]


def pack_kernel(t_ref, g_ref, o0, o1, o2, o3, sems):
    copies = []
    for q, (out, (lat, lon)) in enumerate(zip((o0, o1, o2, o3), quadrants())):
        for i, field in enumerate((t_ref, g_ref)):
            copies.append(pltpu.make_async_copy(field.at[lat, lon], out.at[i], sems.at[q, i]))
    for copy in copies:
        copy.start()
    for copy in copies:
        copy.wait()


def unpack_kernel(p0, p1, p2, p3, mixed_ref, token_ref, sems):
    copies = []
    for q, (piece, (lat, lon)) in enumerate(zip((p0, p1, p2, p3), quadrants())):
        for i, field in enumerate((mixed_ref, token_ref)):
            copies.append(pltpu.make_async_copy(piece.at[i], field.at[lat, lon], sems.at[q, i]))
    for copy in copies:
        copy.start()
    for copy in copies:
        copy.wait()


def stage_kernel(w_ref, held_ref, turned_ref):
    held_ref[...] = w_ref[...]
    turned_ref[...] = w_ref[3 * FEAT :, :].T


def order_matrix(window_axis):
    shape = (2 * WIN, 2 * WIN)
    row = lax.broadcasted_iota(jnp.int32, shape, window_axis)
    col = lax.broadcasted_iota(jnp.int32, shape, 1 - window_axis)
    outer = row >= WIN
    j = jnp.where(outer, row - WIN, row)
    level = j & 1
    source = 4 * (j >> 1) + jnp.where(outer, 3 * level, 1 + level)
    return (source == col).astype(f32).astype(bf16)


def put_rows(core, block, part, kept_ref, sent_ref):
    for h in range(0, HEADS, 2):
        for xl in range(2):
            for zl in range(2):
                two = []
                for c in range(2):
                    at = h * HEAD + zl * 32 + xl * 16 + c * 8
                    pair = [block[at : at + 8], block[at + HEAD : at + HEAD + 8]]
                    two.append(jnp.concatenate(pair, axis=0))
                at = (part * 2 + h // 4) * 128 + xl * 64 + zl * 32 + (h % 4) * 8
                kept_ref[at : at + 16, :] = jnp.where(core == 0, two[0], two[1]).astype(bf16)
                sent_ref[at : at + 16, :] = jnp.where(core == 0, two[1], two[0]).astype(bf16)


def main_kernel(
    p0, p1, p2, p3, w_ref, wot_ref,
    x_ref, g_ref, dqt_ref, dkt_ref, dvt_ref, ctxt_ref, kept_ref, sent_ref,
    rows_ref, s_ref, dp_ref, pb_ref, ds_ref,
):
    core = lax.axis_index("c")
    last = lax.axis_size(LAT) - 1
    seam = lax.axis_index("xh") * 4 + lax.axis_index("y") == jnp.where(core == 0, last, 0)
    order = order_matrix(0)
    fields = []
    for i, ref in enumerate((x_ref, g_ref)):
        for q, piece in enumerate((p0, p1, p2, p3)):
            for a in range(3):
                for b in range(6):
                    at = ((q * 3 + a) * 6 + b) * 4
                    rows_ref[i, at : at + 4, :] = piece[i, a, b].astype(f32)
        field = nn(order, rows_ref[i].astype(bf16))
        fields.append(field)
        ref[...] = field.astype(bf16)
    normed = normalize(fields[0])[0].astype(bf16)
    grad = fields[1].astype(bf16)
    kvn = nt(normed, w_ref[FEAT : 3 * FEAT, :]).astype(bf16)
    key = lax.broadcasted_iota(jnp.int32, (WIN, WIN), 0)
    query = lax.broadcasted_iota(jnp.int32, (WIN, WIN), 1)
    apart = seam & ((key >= 72) != (query >= 72))
    levels = (key & 1) != (query & 1)
    halves = []
    zero = jnp.zeros((HEAD, WIN), bf16)
    for w in range(2):
        rows = slice(w * WIN, (w + 1) * WIN)
        nw = normed[rows]
        qkvt = nt(w_ref[: 3 * FEAT, :], nw).astype(bf16)
        cgt = nt(wot_ref[...], grad[rows]).astype(bf16)
        qt, kt, vt = qkvt[:FEAT], qkvt[FEAT : 2 * FEAT], qkvt[2 * FEAT :]
        halves.append((nw, qt, kt, vt, cgt))
        scaled_q = (qt.astype(f32) * 0.125).astype(bf16)
        scaled_c = (cgt.astype(f32) * 0.125).astype(bf16)
        for h in range(HEADS):
            pair = slice((h // 2) * 128, (h // 2) * 128 + 128)
            value = slice(FEAT + (h // 2) * 128, FEAT + (h // 2) * 128 + 128)
            mine = slice(h * HEAD, h * HEAD + HEAD)

            def padded(half):
                return jnp.concatenate([half, zero] if h % 2 == 0 else [zero, half], axis=0)

            s_ref[w, h] = nn(kvn[rows, pair], padded(scaled_q[mine]))
            dp_ref[w, h] = nn(kvn[rows, value], padded(scaled_c[mine]))
    for w in range(2):
        hidden = apart if w == 0 else apart | levels
        for h in range(HEADS):
            s = jnp.where(hidden, masked_score, s_ref[w, h] * LOG2E)
            e = jnp.exp2(s - jnp.max(s, axis=0, keepdims=True))
            p = e * (1.0 / jnp.sum(e, axis=0, keepdims=True))
            dp = dp_ref[w, h]
            pb_ref[w, h] = p.astype(bf16)
            ds_ref[w, h] = (p * (dp - jnp.sum(dp * p, axis=0, keepdims=True))).astype(bf16)
    for w in range(2):
        nw, qt, kt, vt, cgt = halves[w]
        for h in range(HEADS):
            mine = slice(h * HEAD, h * HEAD + HEAD)
            pb = pb_ref[w, h]
            ds = ds_ref[w, h]
            ctxt_ref[w, mine, :] = nn(vt[mine], pb).astype(bf16)
            dvt_ref[w, mine, :] = nt(cgt[mine], pb).astype(bf16)
            dqt_ref[w, mine, :] = nn(kt[mine], ds).astype(bf16)
            dkt_ref[w, mine, :] = nt(qt[mine], ds).astype(bf16)
    for part, ref in enumerate((dqt_ref, dkt_ref, dvt_ref)):
        block = nn(ref[0], halves[0][0]) + nn(ref[1], halves[1][0])
        put_rows(core, block, part, kept_ref, sent_ref)
    block = nt(grad[:WIN].T, ctxt_ref[0]) + nt(grad[WIN:].T, ctxt_ref[1])
    put_rows(core, block, 3, kept_ref, sent_ref)


def back_kernel(
    x_ref, g_ref, w_ref, dqt_ref, dkt_ref, dvt_ref, ctxt_ref, o0, o1, o2, o3, rows_ref, win_ref
):
    for w in range(2):
        rows = slice(w * WIN, (w + 1) * WIN)
        x = x_ref[rows, :].astype(f32)
        normed_exact, inverse = normalize(x)
        win_ref[0, rows, :] = (x + nt(ctxt_ref[w].T, w_ref[3 * FEAT :, :])).astype(bf16)
        normed_grad = (
            nn(dqt_ref[w].T, w_ref[:FEAT, :])
            + nn(dkt_ref[w].T, w_ref[FEAT : 2 * FEAT, :])
            + nn(dvt_ref[w].T, w_ref[2 * FEAT : 3 * FEAT, :])
        )
        correction = (
            normed_grad
            - jnp.mean(normed_grad, axis=-1, keepdims=True)
            - normed_exact * jnp.mean(normed_grad * normed_exact, axis=-1, keepdims=True)
        )
        win_ref[1, rows, :] = (g_ref[rows, :].astype(f32) + inverse * correction).astype(bf16)
    order = order_matrix(1)
    for i in range(2):
        rows_ref[...] = nn(order, win_ref[i])
        for q, piece in enumerate((o0, o1, o2, o3)):
            for a in range(3):
                for b in range(6):
                    at = ((q * 3 + a) * 6 + b) * 4
                    piece[i, a, b] = rows_ref[at : at + 4, :].astype(bf16)


def shift(piece, lat, lon, back):
    n_lat, n_lon = lax.axis_size(LAT), lax.axis_size(LON)
    pairs = []
    for i in range(n_lat):
        for j in range(n_lon):
            from_lat = (i + (lat if j % 2 == 0 else -lat)) % n_lat
            owner = from_lat * n_lon + (j + lon) % n_lon
            pairs.append((i * n_lon + j, owner) if back else (owner, i * n_lon + j))
    return lax.ppermute(piece, ALL, pairs)


def body(tokens, weights, out_grad):
    quads = [(QUAD, bf16)] * 4
    sems = [pltpu.SemaphoreType.DMA((4, 2))]
    moves = ((0, 1), (1, 0), (1, 1))
    sources = [
        pltpu.with_memory_space_constraint(a.transpose(1, 2, 0, 3), pltpu.HBM)
        for a in (tokens, out_grad)
    ]
    parts = call(pack_kernel, quads, sems, 4, sources, [HBM] * 2)
    parts = [parts[0]] + [shift(p, *m, False) for p, m in zip(parts[1:], moves)]
    wide = ((4 * FEAT, FEAT), bf16)
    held, turned = call(stage_kernel, [wide, ((FEAT, FEAT), bf16)], [], 8, (weights,))
    rows = ((2 * WIN, FEAT), bf16)
    square = ((2, FEAT, WIN), bf16)
    half = ((2 * FEAT, FEAT), bf16)

    def tiles(kind):
        return pltpu.VMEM((2, HEADS, WIN, WIN), kind)

    x, grad, dqt, dkt, dvt, ctxt, kept, sent = call(
        main_kernel,
        [rows] * 2 + [square] * 4 + [half] * 2,
        [pltpu.VMEM((2, 2 * WIN, FEAT), f32)] + [tiles(f32)] * 2 + [tiles(bf16)] * 2,
        20,
        (*parts, held, turned),
    )
    got = lax.ppermute(sent, "c", [(0, 1), (1, 0)])
    backs = call(
        back_kernel,
        quads,
        [pltpu.VMEM((2 * WIN, FEAT), f32), pltpu.VMEM((2, 2 * WIN, FEAT), bf16)],
        12,
        (x, grad, held, dqt, dkt, dvt, ctxt),
    )
    got, backs = lax.optimization_barrier((got, backs))
    total = (kept.astype(f32) + got.astype(f32)).astype(bf16).reshape(32, 32, FEAT)
    total = lax.all_to_all(total, ("xh", "y", "xl", "zl"), 0, 0, tiled=True)
    backs = [backs[0]] + [shift(p, *m, True) for p, m in zip(backs[1:], moves)]
    total = jnp.sum(total.astype(f32), axis=0)
    total, backs[1] = lax.optimization_barrier((total, backs[1]))
    at = lax.axis_index("zh")
    for bit in (2, 1):
        total = total.reshape(2, 8 * bit, FEAT)
        mine = (at // bit) % 2
        gone = lax.dynamic_index_in_dim(total, 1 - mine, 0, keepdims=False)
        held_back = lax.dynamic_index_in_dim(total, mine, 0, keepdims=False)
        total = held_back + lax.ppermute(gone, "zh", [(i, i ^ bit) for i in range(4)])
    weight_grads = total
    field = ((6, 12, 4, FEAT), bf16)
    results = call(unpack_kernel, [field] * 2, sems, 4, backs, [ANY] * 4, HBM)
    mixed, token_grads = (r.transpose(2, 0, 1, 3) for r in results)
    return mixed, token_grads, weight_grads


def solution(mesh):
    fine = Mesh(mesh.devices.reshape(2, 4, 4, 2, 2, 2), ALL)
    spread = P(None, LAT, LON, None)
    return jax.shard_map(
        body,
        mesh=fine,
        in_specs=(spread, P(), spread),
        out_specs=(spread, spread, P(ALL, None)),
        check_vma=False,
    )
```

```python
import jax
import jax.numpy as jnp
from jax import lax
from jax.experimental import pallas as pl
from jax.experimental.pallas import tpu as pltpu
from jax.sharding import Mesh, PartitionSpec as P

HEADS = 8
FEAT = 512
HEAD = 64
WIN = 144
epsilon = 1e-05
masked_score = -1e30
LAT = ("xh", "y")
LON = ("zh", "zl", "xl", "c")
ALL = LAT + LON
VMEM = pl.BlockSpec(memory_space=pltpu.VMEM)
HBM = pl.BlockSpec(memory_space=pltpu.HBM)
ANY = pl.BlockSpec(memory_space=pl.ANY)
LOG2E = 1.4426950408889634
f32 = jnp.float32
bf16 = jnp.bfloat16


def nn(a, b):
    return lax.dot_general(a, b, (((1,), (0,)), ((), ())), preferred_element_type=f32)


def nt(a, b):
    return lax.dot_general(a, b, (((1,), (1,)), ((), ())), preferred_element_type=f32)


def call(kernel, outs, scratch, mib, args, kinds=None, out_kind=VMEM):
    return pl.pallas_call(
        kernel,
        out_shape=[jax.ShapeDtypeStruct(s, d) for s, d in outs],
        in_specs=[VMEM] * len(args) if kinds is None else kinds,
        out_specs=[out_kind] * len(outs),
        scratch_shapes=scratch,
        compiler_params=pltpu.CompilerParams(vmem_limit_bytes=mib * 2**20),
    )(*args)


def normalize(x):
    mean = jnp.mean(x, axis=-1, keepdims=True)
    centred = x - mean
    inverse = lax.rsqrt(jnp.mean(centred * centred, axis=-1, keepdims=True) + epsilon)
    return centred * inverse, inverse


QUAD = (2, 3, 6, 4, FEAT)


def quadrants():
    own = jnp.where(lax.axis_index("c") == lax.axis_index("xl"), 3, 0)
    left = jnp.where(lax.axis_index("xl") == 0, 3, 0)
    return [
        (pl.ds(lat, 3), pl.ds(lon, 6))
        for lat, lon in ((own, 6), (left, 0), (3 - own, 6), (3 - left, 0))
    ]


def pack_kernel(t_ref, g_ref, o0, o1, o2, o3, sems):
    copies = []
    for q, (out, (lat, lon)) in enumerate(zip((o0, o1, o2, o3), quadrants())):
        for i, field in enumerate((t_ref, g_ref)):
            copies.append(pltpu.make_async_copy(field.at[lat, lon], out.at[i], sems.at[q, i]))
    for copy in copies:
        copy.start()
    for copy in copies:
        copy.wait()


def unpack_kernel(p0, p1, p2, p3, mixed_ref, token_ref, sems):
    copies = []
    for q, (piece, (lat, lon)) in enumerate(zip((p0, p1, p2, p3), quadrants())):
        for i, field in enumerate((mixed_ref, token_ref)):
            copies.append(pltpu.make_async_copy(piece.at[i], field.at[lat, lon], sems.at[q, i]))
    for copy in copies:
        copy.start()
    for copy in copies:
        copy.wait()


def stage_kernel(w_ref, held_ref, turned_ref):
    held_ref[...] = w_ref[...]
    turned_ref[...] = w_ref[3 * FEAT :, :].T


def order_matrix(window_axis):
    shape = (2 * WIN, 2 * WIN)
    row = lax.broadcasted_iota(jnp.int32, shape, window_axis)
    col = lax.broadcasted_iota(jnp.int32, shape, 1 - window_axis)
    outer = row >= WIN
    j = jnp.where(outer, row - WIN, row)
    level = j & 1
    source = 4 * (j >> 1) + jnp.where(outer, 3 * level, 1 + level)
    return (source == col).astype(f32).astype(bf16)


def put_rows(core, block, part, kept_ref, sent_ref):
    for h in range(0, HEADS, 2):
        for xl in range(2):
            for zl in range(2):
                two = []
                for c in range(2):
                    at = h * HEAD + zl * 32 + xl * 16 + c * 8
                    pair = [block[at : at + 8], block[at + HEAD : at + HEAD + 8]]
                    two.append(jnp.concatenate(pair, axis=0))
                at = (part * 2 + h // 4) * 128 + xl * 64 + zl * 32 + (h % 4) * 8
                kept_ref[at : at + 16, :] = jnp.where(core == 0, two[0], two[1]).astype(bf16)
                sent_ref[at : at + 16, :] = jnp.where(core == 0, two[1], two[0]).astype(bf16)


def main_kernel(
    p0, p1, p2, p3, w_ref, wot_ref,
    x_ref, g_ref, dqt_ref, dkt_ref, dvt_ref, ctxt_ref, kept_ref, sent_ref,
    rows_ref, s_ref, dp_ref, pb_ref, ds_ref,
):
    core = lax.axis_index("c")
    last = lax.axis_size(LAT) - 1
    upper = core == lax.axis_index("xl")
    seam = lax.axis_index("xh") * 4 + lax.axis_index("y") == jnp.where(upper, last, 0)
    order = order_matrix(0)
    fields = []
    for i, ref in enumerate((x_ref, g_ref)):
        for q, piece in enumerate((p0, p1, p2, p3)):
            for a in range(3):
                for b in range(6):
                    at = ((q * 3 + a) * 6 + b) * 4
                    rows_ref[i, at : at + 4, :] = piece[i, a, b].astype(f32)
        field = nn(order, rows_ref[i].astype(bf16))
        fields.append(field)
        ref[...] = field.astype(bf16)
    normed = normalize(fields[0])[0].astype(bf16)
    grad = fields[1].astype(bf16)
    kvn = nt(normed, w_ref[FEAT : 3 * FEAT, :]).astype(bf16)
    key = lax.broadcasted_iota(jnp.int32, (WIN, WIN), 0)
    query = lax.broadcasted_iota(jnp.int32, (WIN, WIN), 1)
    apart = seam & ((key >= 72) != (query >= 72))
    levels = (key & 1) != (query & 1)
    halves = []
    zero = jnp.zeros((HEAD, WIN), bf16)
    for w in range(2):
        rows = slice(w * WIN, (w + 1) * WIN)
        nw = normed[rows]
        qkvt = nt(w_ref[: 3 * FEAT, :], nw).astype(bf16)
        cgt = nt(wot_ref[...], grad[rows]).astype(bf16)
        qt, kt, vt = qkvt[:FEAT], qkvt[FEAT : 2 * FEAT], qkvt[2 * FEAT :]
        halves.append((nw, qt, kt, vt, cgt))
        scaled_q = (qt.astype(f32) * 0.125).astype(bf16)
        scaled_c = (cgt.astype(f32) * 0.125).astype(bf16)
        for h in range(HEADS):
            pair = slice((h // 2) * 128, (h // 2) * 128 + 128)
            value = slice(FEAT + (h // 2) * 128, FEAT + (h // 2) * 128 + 128)
            mine = slice(h * HEAD, h * HEAD + HEAD)

            def padded(half):
                return jnp.concatenate([half, zero] if h % 2 == 0 else [zero, half], axis=0)

            s_ref[w, h] = nn(kvn[rows, pair], padded(scaled_q[mine]))
            dp_ref[w, h] = nn(kvn[rows, value], padded(scaled_c[mine]))
    for w in range(2):
        hidden = apart if w == 0 else apart | levels
        for h in range(HEADS):
            s = jnp.where(hidden, masked_score, s_ref[w, h] * LOG2E)
            e = jnp.exp2(s - jnp.max(s, axis=0, keepdims=True))
            p = e * (1.0 / jnp.sum(e, axis=0, keepdims=True))
            dp = dp_ref[w, h]
            pb_ref[w, h] = p.astype(bf16)
            ds_ref[w, h] = (p * (dp - jnp.sum(dp * p, axis=0, keepdims=True))).astype(bf16)
    for w in range(2):
        nw, qt, kt, vt, cgt = halves[w]
        for h in range(HEADS):
            mine = slice(h * HEAD, h * HEAD + HEAD)
            pb = pb_ref[w, h]
            ds = ds_ref[w, h]
            ctxt_ref[w, mine, :] = nn(vt[mine], pb).astype(bf16)
            dvt_ref[w, mine, :] = nt(cgt[mine], pb).astype(bf16)
            dqt_ref[w, mine, :] = nn(kt[mine], ds).astype(bf16)
            dkt_ref[w, mine, :] = nt(qt[mine], ds).astype(bf16)
    for part, ref in enumerate((dqt_ref, dkt_ref, dvt_ref)):
        block = nn(ref[0], halves[0][0]) + nn(ref[1], halves[1][0])
        put_rows(core, block, part, kept_ref, sent_ref)
    block = nt(grad[:WIN].T, ctxt_ref[0]) + nt(grad[WIN:].T, ctxt_ref[1])
    put_rows(core, block, 3, kept_ref, sent_ref)


def back_kernel(
    x_ref, g_ref, w_ref, dqt_ref, dkt_ref, dvt_ref, ctxt_ref, o0, o1, o2, o3, rows_ref, win_ref
):
    for w in range(2):
        rows = slice(w * WIN, (w + 1) * WIN)
        x = x_ref[rows, :].astype(f32)
        normed_exact, inverse = normalize(x)
        win_ref[0, rows, :] = (x + nt(ctxt_ref[w].T, w_ref[3 * FEAT :, :])).astype(bf16)
        normed_grad = (
            nn(dqt_ref[w].T, w_ref[:FEAT, :])
            + nn(dkt_ref[w].T, w_ref[FEAT : 2 * FEAT, :])
            + nn(dvt_ref[w].T, w_ref[2 * FEAT : 3 * FEAT, :])
        )
        correction = (
            normed_grad
            - jnp.mean(normed_grad, axis=-1, keepdims=True)
            - normed_exact * jnp.mean(normed_grad * normed_exact, axis=-1, keepdims=True)
        )
        win_ref[1, rows, :] = (g_ref[rows, :].astype(f32) + inverse * correction).astype(bf16)
    order = order_matrix(1)
    for i in range(2):
        rows_ref[...] = nn(order, win_ref[i])
        for q, piece in enumerate((o0, o1, o2, o3)):
            for a in range(3):
                for b in range(6):
                    at = ((q * 3 + a) * 6 + b) * 4
                    piece[i, a, b] = rows_ref[at : at + 4, :].astype(bf16)


def shift(piece, lat, lon, back):
    n_lat, n_lon = lax.axis_size(LAT), lax.axis_size(LON)
    pairs = []
    for i in range(n_lat):
        for j in range(n_lon):
            from_lat = (i + (lat if j % 4 in (0, 3) else -lat)) % n_lat
            owner = from_lat * n_lon + (j + lon) % n_lon
            pairs.append((i * n_lon + j, owner) if back else (owner, i * n_lon + j))
    return lax.ppermute(piece, ALL, pairs)


def body(tokens, weights, out_grad):
    quads = [(QUAD, bf16)] * 4
    sems = [pltpu.SemaphoreType.DMA((4, 2))]
    moves = ((0, 1), (1, 0), (1, 1))
    sources = [
        pltpu.with_memory_space_constraint(a.transpose(1, 2, 0, 3), pltpu.HBM)
        for a in (tokens, out_grad)
    ]
    parts = call(pack_kernel, quads, sems, 4, sources, [HBM] * 2)
    parts = [parts[0]] + [shift(p, *m, False) for p, m in zip(parts[1:], moves)]
    wide = ((4 * FEAT, FEAT), bf16)
    held, turned = call(stage_kernel, [wide, ((FEAT, FEAT), bf16)], [], 8, (weights,))
    rows = ((2 * WIN, FEAT), bf16)
    square = ((2, FEAT, WIN), bf16)
    half = ((2 * FEAT, FEAT), bf16)

    def tiles(kind):
        return pltpu.VMEM((2, HEADS, WIN, WIN), kind)

    x, grad, dqt, dkt, dvt, ctxt, kept, sent = call(
        main_kernel,
        [rows] * 2 + [square] * 4 + [half] * 2,
        [pltpu.VMEM((2, 2 * WIN, FEAT), f32)] + [tiles(f32)] * 2 + [tiles(bf16)] * 2,
        20,
        (*parts, held, turned),
    )
    got = lax.ppermute(sent, "c", [(0, 1), (1, 0)])
    backs = call(
        back_kernel,
        quads,
        [pltpu.VMEM((2 * WIN, FEAT), f32), pltpu.VMEM((2, 2 * WIN, FEAT), bf16)],
        12,
        (x, grad, held, dqt, dkt, dvt, ctxt),
    )
    got, backs = lax.optimization_barrier((got, backs))
    total = (kept.astype(f32) + got.astype(f32)).astype(bf16).reshape(32, 32, FEAT)
    total = lax.all_to_all(total, ("xh", "y", "xl", "zl"), 0, 0, tiled=True)
    backs = [backs[0]] + [shift(p, *m, True) for p, m in zip(backs[1:], moves)]
    total = jnp.sum(total.astype(f32), axis=0)
    total, backs[1], backs[2] = lax.optimization_barrier((total, backs[1], backs[2]))
    at = lax.axis_index("zh")
    for bit in (2, 1):
        total = total.reshape(2, 8 * bit, FEAT)
        mine = (at // bit) % 2
        gone = lax.dynamic_index_in_dim(total, 1 - mine, 0, keepdims=False)
        held_back = lax.dynamic_index_in_dim(total, mine, 0, keepdims=False)
        total = held_back + lax.ppermute(gone, "zh", [(i, i ^ bit) for i in range(4)])
    weight_grads = total
    field = ((6, 12, 4, FEAT), bf16)
    results = call(unpack_kernel, [field] * 2, sems, 4, backs, [ANY] * 4, HBM)
    mixed, token_grads = (r.transpose(2, 0, 1, 3) for r in results)
    return mixed, token_grads, weight_grads


def solution(mesh):
    fine = Mesh(mesh.devices.reshape(2, 4, 4, 2, 2, 2), ALL)
    spread = P(None, LAT, LON, None)
    return jax.shard_map(
        body,
        mesh=fine,
        in_specs=(spread, P(), spread),
        out_specs=(spread, spread, P(ALL, None)),
        check_vma=False,
    )
```

```python
import jax
import jax.numpy as jnp
from jax import lax
from jax.experimental import pallas as pl
from jax.experimental.pallas import tpu as pltpu
from jax.sharding import Mesh, PartitionSpec as P

HEADS = 8
FEAT = 512
HEAD = 64
WIN = 144
epsilon = 1e-05
masked_score = -1e30
LAT = ("xh", "y")
LON = ("zh", "zl", "xl", "c")
ALL = LAT + LON
VMEM = pl.BlockSpec(memory_space=pltpu.VMEM)
HBM = pl.BlockSpec(memory_space=pltpu.HBM)
ANY = pl.BlockSpec(memory_space=pl.ANY)
LOG2E = 1.4426950408889634
f32 = jnp.float32
bf16 = jnp.bfloat16


def nn(a, b):
    return lax.dot_general(a, b, (((1,), (0,)), ((), ())), preferred_element_type=f32)


def nt(a, b):
    return lax.dot_general(a, b, (((1,), (1,)), ((), ())), preferred_element_type=f32)


def call(kernel, outs, scratch, mib, args, kinds=None, out_kind=VMEM):
    return pl.pallas_call(
        kernel,
        out_shape=[jax.ShapeDtypeStruct(s, d) for s, d in outs],
        in_specs=[VMEM] * len(args) if kinds is None else kinds,
        out_specs=[out_kind] * len(outs),
        scratch_shapes=scratch,
        compiler_params=pltpu.CompilerParams(vmem_limit_bytes=mib * 2**20),
    )(*args)


def normalize(x):
    mean = jnp.mean(x, axis=-1, keepdims=True)
    centred = x - mean
    inverse = lax.rsqrt(jnp.mean(centred * centred, axis=-1, keepdims=True) + epsilon)
    return centred * inverse, inverse


QUAD = (2, 3, 6, 4, FEAT)


def quadrants():
    own = jnp.where(lax.axis_index("c") == lax.axis_index("xl"), 3, 0)
    left = jnp.where(lax.axis_index("xl") == 0, 3, 0)
    return [
        (pl.ds(lat, 3), pl.ds(lon, 6))
        for lat, lon in ((own, 6), (left, 0), (3 - own, 6), (3 - left, 0))
    ]


def pack_kernel(t_ref, g_ref, o0, o1, o2, o3, sems):
    copies = []
    for q, (out, (lat, lon)) in enumerate(zip((o0, o1, o2, o3), quadrants())):
        for i, field in enumerate((t_ref, g_ref)):
            copies.append(pltpu.make_async_copy(field.at[lat, lon], out.at[i], sems.at[q, i]))
    for copy in copies:
        copy.start()
    for copy in copies:
        copy.wait()


def unpack_kernel(p0, p1, p2, p3, mixed_ref, token_ref, sems):
    copies = []
    for q, (piece, (lat, lon)) in enumerate(zip((p0, p1, p2, p3), quadrants())):
        for i, field in enumerate((mixed_ref, token_ref)):
            copies.append(pltpu.make_async_copy(piece.at[i], field.at[lat, lon], sems.at[q, i]))
    for copy in copies:
        copy.start()
    for copy in copies:
        copy.wait()


def stage_kernel(w_ref, held_ref, turned_ref, order_ref):
    held_ref[...] = w_ref[...]
    order_ref[...] = order_matrix(0)
    turned_ref[...] = w_ref[3 * FEAT :, :].T


def order_matrix(window_axis):
    shape = (2 * WIN, 2 * WIN)
    row = lax.broadcasted_iota(jnp.int32, shape, window_axis)
    col = lax.broadcasted_iota(jnp.int32, shape, 1 - window_axis)
    outer = row >= WIN
    j = jnp.where(outer, row - WIN, row)
    level = j & 1
    source = 4 * (j >> 1) + jnp.where(outer, 3 * level, 1 + level)
    return (source == col).astype(f32).astype(bf16)


def put_rows(core, block, part, kept_ref, sent_ref):
    for h in range(0, HEADS, 2):
        for xl in range(2):
            for zl in range(2):
                two = []
                for c in range(2):
                    at = h * HEAD + zl * 32 + xl * 16 + c * 8
                    pair = [block[at : at + 8], block[at + HEAD : at + HEAD + 8]]
                    two.append(jnp.concatenate(pair, axis=0))
                at = (part * 2 + h // 4) * 128 + xl * 64 + zl * 32 + (h % 4) * 8
                kept_ref[at : at + 16, :] = jnp.where(core == 0, two[0], two[1]).astype(bf16)
                sent_ref[at : at + 16, :] = jnp.where(core == 0, two[1], two[0]).astype(bf16)


def main_kernel(
    p0, p1, p2, p3, w_ref, wot_ref, order_ref,
    x_ref, g_ref, dqt_ref, dkt_ref, dvt_ref, ctxt_ref, kept_ref, sent_ref,
    rows_ref, s_ref, dp_ref, pb_ref, ds_ref,
):
    core = lax.axis_index("c")
    last = lax.axis_size(LAT) - 1
    upper = core == lax.axis_index("xl")
    seam = lax.axis_index("xh") * 4 + lax.axis_index("y") == jnp.where(upper, last, 0)
    order = order_ref[...]
    fields = []
    for i, ref in enumerate((x_ref, g_ref)):
        for q, piece in enumerate((p0, p1, p2, p3)):
            for a in range(3):
                for b in range(6):
                    at = ((q * 3 + a) * 6 + b) * 4
                    rows_ref[i, at : at + 4, :] = piece[i, a, b].astype(f32)
        field = nn(order, rows_ref[i].astype(bf16))
        fields.append(field)
        ref[...] = field.astype(bf16)
    normed = normalize(fields[0])[0].astype(bf16)
    grad = fields[1].astype(bf16)
    kvn = nt(normed, w_ref[FEAT : 3 * FEAT, :]).astype(bf16)
    key = lax.broadcasted_iota(jnp.int32, (WIN, WIN), 0)
    query = lax.broadcasted_iota(jnp.int32, (WIN, WIN), 1)
    apart = seam & ((key >= 72) != (query >= 72))
    levels = (key & 1) != (query & 1)
    zero = jnp.zeros((HEAD, WIN), bf16)
    halves = []
    for w in range(2):
        nw = normed[w * WIN : (w + 1) * WIN]
        qkvt = nt(w_ref[: 3 * FEAT, :], nw).astype(bf16)
        cgt = nt(wot_ref[...], grad[w * WIN : (w + 1) * WIN]).astype(bf16)
        qt, kt, vt = qkvt[:FEAT], qkvt[FEAT : 2 * FEAT], qkvt[2 * FEAT :]
        scaled_q = (qt.astype(f32) * 0.125).astype(bf16)
        scaled_c = (cgt.astype(f32) * 0.125).astype(bf16)
        halves.append((nw, qt, kt, vt, cgt, scaled_q, scaled_c))

    def scores(w, h):
        rows = slice(w * WIN, (w + 1) * WIN)
        pair = slice((h // 2) * 128, (h // 2) * 128 + 128)
        value = slice(FEAT + (h // 2) * 128, FEAT + (h // 2) * 128 + 128)
        mine = slice(h * HEAD, h * HEAD + HEAD)
        scaled_q, scaled_c = halves[w][5:]

        def padded(half):
            return jnp.concatenate([half, zero] if h % 2 == 0 else [zero, half], axis=0)

        s_ref[w, h] = nn(kvn[rows, pair], padded(scaled_q[mine]))
        dp_ref[w, h] = nn(kvn[rows, value], padded(scaled_c[mine]))

    def softmax(w, h):
        hidden = apart if w == 0 else apart | levels
        s = jnp.where(hidden, masked_score, s_ref[w, h] * LOG2E)
        e = jnp.exp2(s - jnp.max(s, axis=0, keepdims=True))
        p = e * (1.0 / jnp.sum(e, axis=0, keepdims=True))
        dp = dp_ref[w, h]
        pb_ref[w, h] = p.astype(bf16)
        ds_ref[w, h] = (p * (dp - jnp.sum(dp * p, axis=0, keepdims=True))).astype(bf16)

    def products(w, h):
        qt, kt, vt, cgt = halves[w][1:5]
        mine = slice(h * HEAD, h * HEAD + HEAD)
        pb = pb_ref[w, h]
        ds = ds_ref[w, h]
        ctxt_ref[w, mine, :] = nn(vt[mine], pb).astype(bf16)
        dvt_ref[w, mine, :] = nt(cgt[mine], pb).astype(bf16)
        dqt_ref[w, mine, :] = nn(kt[mine], ds).astype(bf16)
        dkt_ref[w, mine, :] = nt(qt[mine], ds).astype(bf16)

    for h in range(HEADS):
        scores(0, h)
    for h in range(HEADS):
        scores(1, h)
        softmax(0, h)
    for h in range(HEADS):
        products(0, h)
        softmax(1, h)
    for h in range(HEADS):
        products(1, h)
    for part, ref in enumerate((dqt_ref, dkt_ref, dvt_ref)):
        block = nn(ref[0], halves[0][0]) + nn(ref[1], halves[1][0])
        put_rows(core, block, part, kept_ref, sent_ref)
    block = nt(grad[:WIN].T, ctxt_ref[0]) + nt(grad[WIN:].T, ctxt_ref[1])
    put_rows(core, block, 3, kept_ref, sent_ref)


def back_kernel(
    x_ref, g_ref, w_ref, dqt_ref, dkt_ref, dvt_ref, ctxt_ref, o0, o1, o2, o3, rows_ref, win_ref
):
    for w in range(2):
        rows = slice(w * WIN, (w + 1) * WIN)
        x = x_ref[rows, :].astype(f32)
        normed_exact, inverse = normalize(x)
        win_ref[0, rows, :] = (x + nt(ctxt_ref[w].T, w_ref[3 * FEAT :, :])).astype(bf16)
        normed_grad = (
            nn(dqt_ref[w].T, w_ref[:FEAT, :])
            + nn(dkt_ref[w].T, w_ref[FEAT : 2 * FEAT, :])
            + nn(dvt_ref[w].T, w_ref[2 * FEAT : 3 * FEAT, :])
        )
        correction = (
            normed_grad
            - jnp.mean(normed_grad, axis=-1, keepdims=True)
            - normed_exact * jnp.mean(normed_grad * normed_exact, axis=-1, keepdims=True)
        )
        win_ref[1, rows, :] = (g_ref[rows, :].astype(f32) + inverse * correction).astype(bf16)
    order = order_matrix(1)
    for i in range(2):
        rows_ref[...] = nn(order, win_ref[i])
        for q, piece in enumerate((o0, o1, o2, o3)):
            for a in range(3):
                for b in range(6):
                    at = ((q * 3 + a) * 6 + b) * 4
                    piece[i, a, b] = rows_ref[at : at + 4, :].astype(bf16)


def shift(piece, lat, lon, back):
    n_lat, n_lon = lax.axis_size(LAT), lax.axis_size(LON)
    pairs = []
    for i in range(n_lat):
        for j in range(n_lon):
            from_lat = (i + (lat if j % 4 in (0, 3) else -lat)) % n_lat
            owner = from_lat * n_lon + (j + lon) % n_lon
            pairs.append((i * n_lon + j, owner) if back else (owner, i * n_lon + j))
    return lax.ppermute(piece, ALL, pairs)


def body(tokens, weights, out_grad):
    quads = [(QUAD, bf16)] * 4
    sems = [pltpu.SemaphoreType.DMA((4, 2))]
    moves = ((0, 1), (1, 0), (1, 1))
    sources = [
        pltpu.with_memory_space_constraint(a.transpose(1, 2, 0, 3), pltpu.HBM)
        for a in (tokens, out_grad)
    ]
    parts = call(pack_kernel, quads, sems, 4, sources, [HBM] * 2)
    parts = [parts[0]] + [shift(p, *m, False) for p, m in zip(parts[1:], moves)]
    wide = ((4 * FEAT, FEAT), bf16)
    square = ((FEAT, FEAT), bf16)
    turn = ((2 * WIN, 2 * WIN), bf16)
    held, turned, order = call(stage_kernel, [wide, square, turn], [], 8, (weights,))
    rows = ((2 * WIN, FEAT), bf16)
    square = ((2, FEAT, WIN), bf16)
    half = ((2 * FEAT, FEAT), bf16)

    def tiles(kind):
        return pltpu.VMEM((2, HEADS, WIN, WIN), kind)

    x, grad, dqt, dkt, dvt, ctxt, kept, sent = call(
        main_kernel,
        [rows] * 2 + [square] * 4 + [half] * 2,
        [pltpu.VMEM((2, 2 * WIN, FEAT), f32)] + [tiles(f32)] * 2 + [tiles(bf16)] * 2,
        20,
        (*parts, held, turned, order),
    )
    got = lax.ppermute(sent, "c", [(0, 1), (1, 0)])
    backs = call(
        back_kernel,
        quads,
        [pltpu.VMEM((2 * WIN, FEAT), f32), pltpu.VMEM((2, 2 * WIN, FEAT), bf16)],
        12,
        (x, grad, held, dqt, dkt, dvt, ctxt),
    )
    got, backs = lax.optimization_barrier((got, backs))
    total = (kept.astype(f32) + got.astype(f32)).astype(bf16).reshape(32, 32, FEAT)
    total = lax.all_to_all(total, ("xh", "y", "xl", "zl"), 0, 0, tiled=True)
    backs = [backs[0]] + [shift(p, *m, True) for p, m in zip(backs[1:], moves)]
    total = jnp.sum(total.astype(f32), axis=0)
    total, backs[2], backs[3] = lax.optimization_barrier((total, backs[2], backs[3]))
    at = lax.axis_index("zh")
    for bit in (2, 1):
        total = total.reshape(2, 8 * bit, FEAT)
        mine = (at // bit) % 2
        gone = lax.dynamic_index_in_dim(total, 1 - mine, 0, keepdims=False)
        held_back = lax.dynamic_index_in_dim(total, mine, 0, keepdims=False)
        total = held_back + lax.ppermute(gone, "zh", [(i, i ^ bit) for i in range(4)])
    weight_grads = total
    field = ((6, 12, 4, FEAT), bf16)
    results = call(unpack_kernel, [field] * 2, sems, 4, backs, [ANY] * 4, HBM)
    mixed, token_grads = (r.transpose(2, 0, 1, 3) for r in results)
    return mixed, token_grads, weight_grads


def solution(mesh):
    fine = Mesh(mesh.devices.reshape(2, 4, 4, 2, 2, 2), ALL)
    spread = P(None, LAT, LON, None)
    return jax.shard_map(
        body,
        mesh=fine,
        in_specs=(spread, P(), spread),
        out_specs=(spread, spread, P(ALL, None)),
        check_vma=False,
    )
```

```python
import jax
import jax.numpy as jnp
from jax import lax
from jax.experimental import pallas as pl
from jax.experimental.pallas import tpu as pltpu
from jax.sharding import Mesh, PartitionSpec as P

HEADS = 8
FEAT = 512
HEAD = 64
WIN = 144
epsilon = 1e-05
masked_score = -1e30
LAT = ("xh", "y")
LON = ("zh", "zl", "xl", "c")
ALL = LAT + LON
VMEM = pl.BlockSpec(memory_space=pltpu.VMEM)
HBM = pl.BlockSpec(memory_space=pltpu.HBM)
ANY = pl.BlockSpec(memory_space=pl.ANY)
LOG2E = 1.4426950408889634
f32 = jnp.float32
bf16 = jnp.bfloat16


def nn(a, b):
    return lax.dot_general(a, b, (((1,), (0,)), ((), ())), preferred_element_type=f32)


def nt(a, b):
    return lax.dot_general(a, b, (((1,), (1,)), ((), ())), preferred_element_type=f32)


def call(kernel, outs, scratch, mib, args, kinds=None, out_kind=VMEM):
    return pl.pallas_call(
        kernel,
        out_shape=[jax.ShapeDtypeStruct(s, d) for s, d in outs],
        in_specs=[VMEM] * len(args) if kinds is None else kinds,
        out_specs=[out_kind] * len(outs),
        scratch_shapes=scratch,
        compiler_params=pltpu.CompilerParams(vmem_limit_bytes=mib * 2**20),
    )(*args)


def normalize(x):
    mean = jnp.mean(x, axis=-1, keepdims=True)
    centred = x - mean
    inverse = lax.rsqrt(jnp.mean(centred * centred, axis=-1, keepdims=True) + epsilon)
    return centred * inverse, inverse


QUAD = (2, 3, 6, 4, FEAT)


def quadrants():
    own = jnp.where(lax.axis_index("c") == lax.axis_index("xl"), 3, 0)
    left = jnp.where(lax.axis_index("xl") == 0, 3, 0)
    return [
        (pl.ds(lat, 3), pl.ds(lon, 6))
        for lat, lon in ((own, 6), (left, 0), (3 - own, 6), (3 - left, 0))
    ]


def pack_kernel(t_ref, g_ref, o0, o1, o2, o3, sems):
    copies = []
    for q, (out, (lat, lon)) in enumerate(zip((o0, o1, o2, o3), quadrants())):
        for i, field in enumerate((t_ref, g_ref)):
            copies.append(pltpu.make_async_copy(field.at[lat, lon], out.at[i], sems.at[q, i]))
    for copy in copies:
        copy.start()
    for copy in copies:
        copy.wait()


def unpack_kernel(p0, p1, p2, p3, mixed_ref, token_ref, sems):
    copies = []
    for q, (piece, (lat, lon)) in enumerate(zip((p0, p1, p2, p3), quadrants())):
        for i, field in enumerate((mixed_ref, token_ref)):
            copies.append(pltpu.make_async_copy(piece.at[i], field.at[lat, lon], sems.at[q, i]))
    for copy in copies:
        copy.start()
    for copy in copies:
        copy.wait()


def stage_kernel(w_ref, held_ref, turned_ref, order_ref):
    held_ref[...] = w_ref[...]
    order_ref[...] = order_matrix(0)
    turned_ref[...] = w_ref[3 * FEAT :, :].T


def order_matrix(window_axis):
    shape = (2 * WIN, 2 * WIN)
    row = lax.broadcasted_iota(jnp.int32, shape, window_axis)
    col = lax.broadcasted_iota(jnp.int32, shape, 1 - window_axis)
    outer = row >= WIN
    j = jnp.where(outer, row - WIN, row)
    level = j & 1
    source = 4 * (j >> 1) + jnp.where(outer, 3 * level, 1 + level)
    return (source == col).astype(f32).astype(bf16)


def put_rows(core, block, part, kept_ref, sent_ref):
    for h in range(0, HEADS, 2):
        for xl in range(2):
            for zl in range(2):
                two = []
                for c in range(2):
                    at = h * HEAD + zl * 32 + xl * 16 + c * 8
                    pair = [block[at : at + 8], block[at + HEAD : at + HEAD + 8]]
                    two.append(jnp.concatenate(pair, axis=0))
                at = (part * 2 + h // 4) * 128 + xl * 64 + zl * 32 + (h % 4) * 8
                kept_ref[at : at + 16, :] = jnp.where(core == 0, two[0], two[1]).astype(bf16)
                sent_ref[at : at + 16, :] = jnp.where(core == 0, two[1], two[0]).astype(bf16)


def main_kernel(
    p2, p3, p1, p0, w_ref, wot_ref, order_ref,
    x_ref, g_ref, dqt_ref, dkt_ref, dvt_ref, ctxt_ref, kept_ref, sent_ref,
    rows_ref, s_ref, dp_ref, pb_ref, ds_ref,
):
    core = lax.axis_index("c")
    last = lax.axis_size(LAT) - 1
    upper = core == lax.axis_index("xl")
    seam = lax.axis_index("xh") * 4 + lax.axis_index("y") == jnp.where(upper, last, 0)
    order = order_ref[...]
    fields = []
    for i, ref in enumerate((x_ref, g_ref)):
        for q, piece in enumerate((p0, p1, p2, p3)):
            for a in range(3):
                for b in range(6):
                    at = ((q * 3 + a) * 6 + b) * 4
                    rows_ref[i, at : at + 4, :] = piece[i, a, b].astype(f32)
        field = nn(order, rows_ref[i].astype(bf16))
        fields.append(field)
        ref[...] = field.astype(bf16)
    normed = normalize(fields[0])[0].astype(bf16)
    grad = fields[1].astype(bf16)
    kvn = nt(normed, w_ref[FEAT : 3 * FEAT, :]).astype(bf16)
    key = lax.broadcasted_iota(jnp.int32, (WIN, WIN), 0)
    query = lax.broadcasted_iota(jnp.int32, (WIN, WIN), 1)
    apart = seam & ((key >= 72) != (query >= 72))
    levels = (key & 1) != (query & 1)
    zero = jnp.zeros((HEAD, WIN), bf16)
    halves = []
    for w in range(2):
        nw = normed[w * WIN : (w + 1) * WIN]
        qkvt = nt(w_ref[: 3 * FEAT, :], nw).astype(bf16)
        cgt = nt(wot_ref[...], grad[w * WIN : (w + 1) * WIN]).astype(bf16)
        qt, kt, vt = qkvt[:FEAT], qkvt[FEAT : 2 * FEAT], qkvt[2 * FEAT :]
        scaled_q = (qt.astype(f32) * 0.125).astype(bf16)
        scaled_c = (cgt.astype(f32) * 0.125).astype(bf16)
        halves.append((nw, qt, kt, vt, cgt, scaled_q, scaled_c))

    def scores(w, h):
        rows = slice(w * WIN, (w + 1) * WIN)
        pair = slice((h // 2) * 128, (h // 2) * 128 + 128)
        value = slice(FEAT + (h // 2) * 128, FEAT + (h // 2) * 128 + 128)
        mine = slice(h * HEAD, h * HEAD + HEAD)
        scaled_q, scaled_c = halves[w][5:]

        def padded(half):
            return jnp.concatenate([half, zero] if h % 2 == 0 else [zero, half], axis=0)

        s_ref[w, h] = nn(kvn[rows, pair], padded(scaled_q[mine]))
        dp_ref[w, h] = nn(kvn[rows, value], padded(scaled_c[mine]))

    def softmax(w, h):
        hidden = apart if w == 0 else apart | levels
        s = jnp.where(hidden, masked_score, s_ref[w, h] * LOG2E)
        e = jnp.exp2(s - jnp.max(s, axis=0, keepdims=True))
        p = e * (1.0 / jnp.sum(e, axis=0, keepdims=True))
        dp = dp_ref[w, h]
        pb_ref[w, h] = p.astype(bf16)
        ds_ref[w, h] = (p * (dp - jnp.sum(dp * p, axis=0, keepdims=True))).astype(bf16)

    def products(w, h):
        qt, kt, vt, cgt = halves[w][1:5]
        mine = slice(h * HEAD, h * HEAD + HEAD)
        pb = pb_ref[w, h]
        ds = ds_ref[w, h]
        ctxt_ref[w, mine, :] = nn(vt[mine], pb).astype(bf16)
        dvt_ref[w, mine, :] = nt(cgt[mine], pb).astype(bf16)
        dqt_ref[w, mine, :] = nn(kt[mine], ds).astype(bf16)
        dkt_ref[w, mine, :] = nt(qt[mine], ds).astype(bf16)

    for h in range(HEADS):
        scores(0, h)
    for h in range(HEADS):
        scores(1, h)
        softmax(0, h)
    for h in range(HEADS):
        products(0, h)
        softmax(1, h)
    for h in range(HEADS):
        products(1, h)
    for part, ref in enumerate((dqt_ref, dkt_ref, dvt_ref)):
        block = nn(ref[0], halves[0][0]) + nn(ref[1], halves[1][0])
        put_rows(core, block, part, kept_ref, sent_ref)
    block = nt(grad[:WIN].T, ctxt_ref[0]) + nt(grad[WIN:].T, ctxt_ref[1])
    put_rows(core, block, 3, kept_ref, sent_ref)


def back_kernel(
    x_ref, g_ref, w_ref, dqt_ref, dkt_ref, dvt_ref, ctxt_ref, o0, o1, o2, o3, rows_ref, win_ref
):
    for w in range(2):
        rows = slice(w * WIN, (w + 1) * WIN)
        x = x_ref[rows, :].astype(f32)
        normed_exact, inverse = normalize(x)
        win_ref[0, rows, :] = (x + nt(ctxt_ref[w].T, w_ref[3 * FEAT :, :])).astype(bf16)
        normed_grad = (
            nn(dqt_ref[w].T, w_ref[:FEAT, :])
            + nn(dkt_ref[w].T, w_ref[FEAT : 2 * FEAT, :])
            + nn(dvt_ref[w].T, w_ref[2 * FEAT : 3 * FEAT, :])
        )
        correction = (
            normed_grad
            - jnp.mean(normed_grad, axis=-1, keepdims=True)
            - normed_exact * jnp.mean(normed_grad * normed_exact, axis=-1, keepdims=True)
        )
        win_ref[1, rows, :] = (g_ref[rows, :].astype(f32) + inverse * correction).astype(bf16)
    order = order_matrix(1)
    for i in range(2):
        rows_ref[...] = nn(order, win_ref[i])
        for q, piece in enumerate((o0, o1, o2, o3)):
            for a in range(3):
                for b in range(6):
                    at = ((q * 3 + a) * 6 + b) * 4
                    piece[i, a, b] = rows_ref[at : at + 4, :].astype(bf16)


def shift(piece, lat, lon, back):
    n_lat, n_lon = lax.axis_size(LAT), lax.axis_size(LON)
    pairs = []
    for i in range(n_lat):
        for j in range(n_lon):
            from_lat = (i + (lat if j % 4 in (0, 3) else -lat)) % n_lat
            owner = from_lat * n_lon + (j + lon) % n_lon
            pairs.append((i * n_lon + j, owner) if back else (owner, i * n_lon + j))
    return lax.ppermute(piece, ALL, pairs)


def body(tokens, weights, out_grad):
    quads = [(QUAD, bf16)] * 4
    sems = [pltpu.SemaphoreType.DMA((4, 2))]
    moves = ((0, 0), (0, 1), (1, 0), (1, 1))
    sources = [
        pltpu.with_memory_space_constraint(a.transpose(1, 2, 0, 3), pltpu.HBM)
        for a in (tokens, out_grad)
    ]
    parts = list(call(pack_kernel, quads, sems, 4, sources, [HBM] * 2))
    for q in (2, 3, 1):
        parts[q] = shift(parts[q], *moves[q], False)
    wide = ((4 * FEAT, FEAT), bf16)
    square = ((FEAT, FEAT), bf16)
    turn = ((2 * WIN, 2 * WIN), bf16)
    held, turned, order = call(stage_kernel, [wide, square, turn], [], 8, (weights,))
    rows = ((2 * WIN, FEAT), bf16)
    square = ((2, FEAT, WIN), bf16)
    half = ((2 * FEAT, FEAT), bf16)

    def tiles(kind):
        return pltpu.VMEM((2, HEADS, WIN, WIN), kind)

    x, grad, dqt, dkt, dvt, ctxt, kept, sent = call(
        main_kernel,
        [rows] * 2 + [square] * 4 + [half] * 2,
        [pltpu.VMEM((2, 2 * WIN, FEAT), f32)] + [tiles(f32)] * 2 + [tiles(bf16)] * 2,
        20,
        (parts[2], parts[3], parts[1], parts[0], held, turned, order),
    )
    got = lax.ppermute(sent, "c", [(0, 1), (1, 0)])
    backs = call(
        back_kernel,
        quads,
        [pltpu.VMEM((2 * WIN, FEAT), f32), pltpu.VMEM((2, 2 * WIN, FEAT), bf16)],
        12,
        (x, grad, held, dqt, dkt, dvt, ctxt),
    )
    got, backs = lax.optimization_barrier((got, list(backs)))
    total = (kept.astype(f32) + got.astype(f32)).astype(bf16).reshape(32, 32, FEAT)
    total = lax.all_to_all(total, ("xh", "y", "xl", "zl"), 0, 0, tiled=True)
    for q in (2, 3, 1):
        backs[q] = shift(backs[q], *moves[q], True)
    total = jnp.sum(total.astype(f32), axis=0)
    total, backs[2], backs[3] = lax.optimization_barrier((total, backs[2], backs[3]))
    total = total.reshape(4, 8, FEAT)
    at = lax.axis_index("zh")
    chunks = [lax.dynamic_index_in_dim(total, (at + d) % 4, 0, keepdims=False) for d in range(4)]
    for d in (2, 1, 3):
        pairs = [(i, (i + d) % 4) for i in range(4)]
        chunks[d] = lax.ppermute(chunks[d], "zh", pairs)
    weight_grads = chunks[0] + chunks[2] + (chunks[1] + chunks[3])
    field = ((6, 12, 4, FEAT), bf16)
    results = call(unpack_kernel, [field] * 2, sems, 4, backs, [ANY] * 4, HBM)
    mixed, token_grads = (r.transpose(2, 0, 1, 3) for r in results)
    return mixed, token_grads, weight_grads


def solution(mesh):
    fine = Mesh(mesh.devices.reshape(2, 4, 4, 2, 2, 2), ALL)
    spread = P(None, LAT, LON, None)
    return jax.shard_map(
        body,
        mesh=fine,
        in_specs=(spread, P(), spread),
        out_specs=(spread, spread, P(ALL, None)),
        check_vma=False,
    )
```

```python
import jax
import jax.numpy as jnp
from jax import lax
from jax.experimental import pallas as pl
from jax.experimental.pallas import tpu as pltpu
from jax.sharding import Mesh, PartitionSpec as P

HEADS = 8
FEAT = 512
HEAD = 64
WIN = 144
epsilon = 1e-05
masked_score = -1e30
LAT = ("xh", "y")
LON = ("zh", "zl", "xl", "c")
ALL = LAT + LON
VMEM = pl.BlockSpec(memory_space=pltpu.VMEM)
HBM = pl.BlockSpec(memory_space=pltpu.HBM)
ANY = pl.BlockSpec(memory_space=pl.ANY)
LOG2E = 1.4426950408889634
f32 = jnp.float32
bf16 = jnp.bfloat16


def nn(a, b):
    return lax.dot_general(a, b, (((1,), (0,)), ((), ())), preferred_element_type=f32)


def nt(a, b):
    return lax.dot_general(a, b, (((1,), (1,)), ((), ())), preferred_element_type=f32)


def call(kernel, outs, scratch, mib, args, kinds=None, out_kind=VMEM):
    return pl.pallas_call(
        kernel,
        out_shape=[jax.ShapeDtypeStruct(s, d) for s, d in outs],
        in_specs=[VMEM] * len(args) if kinds is None else kinds,
        out_specs=[out_kind] * len(outs),
        scratch_shapes=scratch,
        compiler_params=pltpu.CompilerParams(vmem_limit_bytes=mib * 2**20),
    )(*args)


def normalize(x):
    mean = jnp.mean(x, axis=-1, keepdims=True)
    centred = x - mean
    inverse = lax.rsqrt(jnp.mean(centred * centred, axis=-1, keepdims=True) + epsilon)
    return centred * inverse, inverse


QUAD = (2, 3, 6, 4, FEAT)


def quadrants():
    own = jnp.where(lax.axis_index("c") == lax.axis_index("xl"), 3, 0)
    left = jnp.where(lax.axis_index("xl") == 0, 3, 0)
    return [
        (pl.ds(lat, 3), pl.ds(lon, 6))
        for lat, lon in ((own, 6), (left, 0), (3 - own, 6), (3 - left, 0))
    ]


def pack_kernel(t_ref, g_ref, o0, o1, o2, o3, sems):
    copies = []
    for q, (out, (lat, lon)) in enumerate(zip((o0, o1, o2, o3), quadrants())):
        for i, field in enumerate((t_ref, g_ref)):
            copies.append(pltpu.make_async_copy(field.at[lat, lon], out.at[i], sems.at[q, i]))
    for copy in copies:
        copy.start()
    for copy in copies:
        copy.wait()


def unpack_kernel(p0, p1, p2, p3, mixed_ref, token_ref, sems):
    copies = []
    for q, (piece, (lat, lon)) in enumerate(zip((p0, p1, p2, p3), quadrants())):
        for i, field in enumerate((mixed_ref, token_ref)):
            copies.append(pltpu.make_async_copy(piece.at[i], field.at[lat, lon], sems.at[q, i]))
    for copy in copies:
        copy.start()
    for copy in copies:
        copy.wait()


def stage_kernel(w_ref, held_ref, turned_ref, order_ref):
    held_ref[...] = w_ref[...]
    order_ref[...] = order_matrix(0)
    turned_ref[...] = w_ref[3 * FEAT :, :].T


def order_matrix(window_axis):
    shape = (2 * WIN, 2 * WIN)
    row = lax.broadcasted_iota(jnp.int32, shape, window_axis)
    col = lax.broadcasted_iota(jnp.int32, shape, 1 - window_axis)
    outer = row >= WIN
    j = jnp.where(outer, row - WIN, row)
    level = j & 1
    source = 4 * (j >> 1) + jnp.where(outer, 3 * level, 1 + level)
    return (source == col).astype(f32).astype(bf16)


def put_rows(core, block, part, kept_ref, sent_ref):
    for h in range(0, HEADS, 2):
        for xl in range(2):
            for zl in range(2):
                two = []
                for c in range(2):
                    at = h * HEAD + zl * 32 + xl * 16 + c * 8
                    pair = [block[at : at + 8], block[at + HEAD : at + HEAD + 8]]
                    two.append(jnp.concatenate(pair, axis=0))
                at = (part * 2 + h // 4) * 128 + xl * 64 + zl * 32 + (h % 4) * 8
                kept_ref[at : at + 16, :] = jnp.where(core == 0, two[0], two[1]).astype(bf16)
                sent_ref[at : at + 16, :] = jnp.where(core == 0, two[1], two[0]).astype(bf16)


def main_kernel(
    p2, p3, p1, p0, w_ref, wot_ref, order_ref,
    x_ref, g_ref, dqt_ref, dkt_ref, dvt_ref, ctxt_ref, kept_ref, sent_ref,
    rows_ref, s_ref, dp_ref, pb_ref, ds_ref,
):
    core = lax.axis_index("c")
    last = lax.axis_size(LAT) - 1
    upper = core == lax.axis_index("xl")
    seam = lax.axis_index("xh") * 4 + lax.axis_index("y") == jnp.where(upper, last, 0)
    order = order_ref[...]
    fields = []
    for i, ref in enumerate((x_ref, g_ref)):
        for q, piece in enumerate((p0, p1, p2, p3)):
            for a in range(3):
                for b in range(6):
                    at = ((q * 3 + a) * 6 + b) * 4
                    rows_ref[i, at : at + 4, :] = piece[i, a, b].astype(f32)
        field = nn(order, rows_ref[i].astype(bf16))
        fields.append(field)
        ref[...] = field.astype(bf16)
    normed = normalize(fields[0])[0].astype(bf16)
    grad = fields[1].astype(bf16)
    kvn = nt(normed, w_ref[FEAT : 3 * FEAT, :]).astype(bf16)
    key = lax.broadcasted_iota(jnp.int32, (WIN, WIN), 0)
    query = lax.broadcasted_iota(jnp.int32, (WIN, WIN), 1)
    apart = seam & ((key >= 72) != (query >= 72))
    levels = (key & 1) != (query & 1)
    zero = jnp.zeros((HEAD, WIN), bf16)
    halves = []
    for w in range(2):
        nw = normed[w * WIN : (w + 1) * WIN]
        qkvt = nt(w_ref[: 3 * FEAT, :], nw).astype(bf16)
        cgt = nt(wot_ref[...], grad[w * WIN : (w + 1) * WIN]).astype(bf16)
        qt, kt, vt = qkvt[:FEAT], qkvt[FEAT : 2 * FEAT], qkvt[2 * FEAT :]
        scaled_q = (qt.astype(f32) * 0.125).astype(bf16)
        scaled_c = (cgt.astype(f32) * 0.125).astype(bf16)
        halves.append((nw, qt, kt, vt, cgt, scaled_q, scaled_c))

    def scores(w, h):
        rows = slice(w * WIN, (w + 1) * WIN)
        pair = slice((h // 2) * 128, (h // 2) * 128 + 128)
        value = slice(FEAT + (h // 2) * 128, FEAT + (h // 2) * 128 + 128)
        mine = slice(h * HEAD, h * HEAD + HEAD)
        scaled_q, scaled_c = halves[w][5:]

        def padded(half):
            return jnp.concatenate([half, zero] if h % 2 == 0 else [zero, half], axis=0)

        s_ref[w, h] = nn(kvn[rows, pair], padded(scaled_q[mine]))
        dp_ref[w, h] = nn(kvn[rows, value], padded(scaled_c[mine]))

    def softmax(w, h):
        hidden = apart if w == 0 else apart | levels
        s = jnp.where(hidden, masked_score, s_ref[w, h] * LOG2E)
        e = jnp.exp2(s - jnp.max(s, axis=0, keepdims=True))
        p = e * (1.0 / jnp.sum(e, axis=0, keepdims=True))
        dp = dp_ref[w, h]
        pb_ref[w, h] = p.astype(bf16)
        ds_ref[w, h] = (p * (dp - jnp.sum(dp * p, axis=0, keepdims=True))).astype(bf16)

    def products(w, h):
        qt, kt, vt, cgt = halves[w][1:5]
        mine = slice(h * HEAD, h * HEAD + HEAD)
        pb = pb_ref[w, h]
        ds = ds_ref[w, h]
        ctxt_ref[w, mine, :] = nn(vt[mine], pb).astype(bf16)
        dvt_ref[w, mine, :] = nt(cgt[mine], pb).astype(bf16)
        dqt_ref[w, mine, :] = nn(kt[mine], ds).astype(bf16)
        dkt_ref[w, mine, :] = nt(qt[mine], ds).astype(bf16)

    for h in range(HEADS):
        scores(0, h)
    for h in range(HEADS):
        scores(1, h)
        softmax(0, h)
    for h in range(HEADS):
        products(0, h)
        softmax(1, h)
    for h in range(HEADS):
        products(1, h)
    for part, ref in enumerate((dqt_ref, dkt_ref, dvt_ref)):
        block = nn(ref[0], halves[0][0]) + nn(ref[1], halves[1][0])
        put_rows(core, block, part, kept_ref, sent_ref)
    block = nt(grad[:WIN].T, ctxt_ref[0]) + nt(grad[WIN:].T, ctxt_ref[1])
    put_rows(core, block, 3, kept_ref, sent_ref)


def back_kernel(
    x_ref, g_ref, w_ref, dqt_ref, dkt_ref, dvt_ref, ctxt_ref, o0, o1, o2, o3, rows_ref, win_ref
):
    for w in range(2):
        rows = slice(w * WIN, (w + 1) * WIN)
        x = x_ref[rows, :].astype(f32)
        normed_exact, inverse = normalize(x)
        win_ref[0, rows, :] = (x + nt(ctxt_ref[w].T, w_ref[3 * FEAT :, :])).astype(bf16)
        normed_grad = (
            nn(dqt_ref[w].T, w_ref[:FEAT, :])
            + nn(dkt_ref[w].T, w_ref[FEAT : 2 * FEAT, :])
            + nn(dvt_ref[w].T, w_ref[2 * FEAT : 3 * FEAT, :])
        )
        correction = (
            normed_grad
            - jnp.mean(normed_grad, axis=-1, keepdims=True)
            - normed_exact * jnp.mean(normed_grad * normed_exact, axis=-1, keepdims=True)
        )
        win_ref[1, rows, :] = (g_ref[rows, :].astype(f32) + inverse * correction).astype(bf16)
    order = order_matrix(1)
    for i in range(2):
        rows_ref[...] = nn(order, win_ref[i])
        for q, piece in enumerate((o0, o1, o2, o3)):
            for a in range(3):
                for b in range(6):
                    at = ((q * 3 + a) * 6 + b) * 4
                    piece[i, a, b] = rows_ref[at : at + 4, :].astype(bf16)


def shift(piece, lat, lon, back):
    n_lat, n_lon = lax.axis_size(LAT), lax.axis_size(LON)
    pairs = []
    for i in range(n_lat):
        for j in range(n_lon):
            from_lat = (i + (lat if j % 4 in (0, 3) else -lat)) % n_lat
            owner = from_lat * n_lon + (j + lon) % n_lon
            pairs.append((i * n_lon + j, owner) if back else (owner, i * n_lon + j))
    return lax.ppermute(piece, ALL, pairs)


def body(tokens, weights, out_grad):
    quads = [(QUAD, bf16)] * 4
    sems = [pltpu.SemaphoreType.DMA((4, 2))]
    moves = ((0, 0), (0, 1), (1, 0), (1, 1))
    sources = [
        pltpu.with_memory_space_constraint(a.transpose(1, 2, 0, 3), pltpu.HBM)
        for a in (tokens, out_grad)
    ]
    parts = list(call(pack_kernel, quads, sems, 4, sources, [HBM] * 2))
    for q in (2, 3, 1):
        parts[q] = shift(parts[q], *moves[q], False)
    wide = ((4 * FEAT, FEAT), bf16)
    square = ((FEAT, FEAT), bf16)
    turn = ((2 * WIN, 2 * WIN), bf16)
    held, turned, order = call(stage_kernel, [wide, square, turn], [], 8, (weights,))
    rows = ((2 * WIN, FEAT), bf16)
    square = ((2, FEAT, WIN), bf16)
    half = ((2 * FEAT, FEAT), bf16)

    def tiles(kind):
        return pltpu.VMEM((2, HEADS, WIN, WIN), kind)

    x, grad, dqt, dkt, dvt, ctxt, kept, sent = call(
        main_kernel,
        [rows] * 2 + [square] * 4 + [half] * 2,
        [pltpu.VMEM((2, 2 * WIN, FEAT), f32)] + [tiles(f32)] * 2 + [tiles(bf16)] * 2,
        20,
        (parts[2], parts[3], parts[1], parts[0], held, turned, order),
    )
    got = lax.ppermute(sent, "c", [(0, 1), (1, 0)])
    backs = call(
        back_kernel,
        quads,
        [pltpu.VMEM((2 * WIN, FEAT), f32), pltpu.VMEM((2, 2 * WIN, FEAT), bf16)],
        12,
        (x, grad, held, dqt, dkt, dvt, ctxt),
    )
    got, backs = lax.optimization_barrier((got, list(backs)))
    total = (kept.astype(f32) + got.astype(f32)).astype(bf16).reshape(32, 32, FEAT)
    total = lax.all_to_all(total, ("xh", "y", "xl", "zl"), 0, 0, tiled=True)
    for q in (2, 3, 1):
        backs[q] = shift(backs[q], *moves[q], True)
    total = jnp.sum(total.astype(f32), axis=0)
    total = total.reshape(4, 8, FEAT)
    at = lax.axis_index("zh")
    chunks = [lax.dynamic_index_in_dim(total, (at + d) % 4, 0, keepdims=False) for d in range(4)]
    for d in (2, 1, 3):
        pairs = [(i, (i + d) % 4) for i in range(4)]
        chunks[d] = lax.ppermute(chunks[d], "zh", pairs)
    field = ((6, 12, 4, FEAT), bf16)
    results = call(unpack_kernel, [field] * 2, sems, 4, backs, [ANY] * 4, HBM)
    chunks, results = lax.optimization_barrier((chunks, results))
    weight_grads = chunks[0] + chunks[2] + (chunks[1] + chunks[3])
    mixed, token_grads = (r.transpose(2, 0, 1, 3) for r in results)
    return mixed, token_grads, weight_grads


def solution(mesh):
    fine = Mesh(mesh.devices.reshape(2, 4, 4, 2, 2, 2), ALL)
    spread = P(None, LAT, LON, None)
    return jax.shard_map(
        body,
        mesh=fine,
        in_specs=(spread, P(), spread),
        out_specs=(spread, spread, P(ALL, None)),
        check_vma=False,
    )
```

```python
import jax
import jax.numpy as jnp
from jax import lax
from jax.experimental import pallas as pl
from jax.experimental.pallas import tpu as pltpu
from jax.sharding import Mesh, PartitionSpec as P

HEADS = 8
FEAT = 512
HEAD = 64
WIN = 144
epsilon = 1e-05
masked_score = -1e30
LAT = ("xh", "y")
LON = ("zh", "zl", "xl", "c")
ALL = LAT + LON
VMEM = pl.BlockSpec(memory_space=pltpu.VMEM)
HBM = pl.BlockSpec(memory_space=pltpu.HBM)
ANY = pl.BlockSpec(memory_space=pl.ANY)
LOG2E = 1.4426950408889634
f32 = jnp.float32
bf16 = jnp.bfloat16


def nn(a, b):
    return lax.dot_general(a, b, (((1,), (0,)), ((), ())), preferred_element_type=f32)


def nt(a, b):
    return lax.dot_general(a, b, (((1,), (1,)), ((), ())), preferred_element_type=f32)


def call(kernel, outs, scratch, mib, args, kinds=None, out_kind=VMEM):
    return pl.pallas_call(
        kernel,
        out_shape=[jax.ShapeDtypeStruct(s, d) for s, d in outs],
        in_specs=[VMEM] * len(args) if kinds is None else kinds,
        out_specs=[out_kind] * len(outs),
        scratch_shapes=scratch,
        compiler_params=pltpu.CompilerParams(vmem_limit_bytes=mib * 2**20),
    )(*args)


def normalize(x):
    mean = jnp.mean(x, axis=-1, keepdims=True)
    centred = x - mean
    inverse = lax.rsqrt(jnp.mean(centred * centred, axis=-1, keepdims=True) + epsilon)
    return centred * inverse, inverse


QUAD = (2, 3, 6, 4, FEAT)


def quadrants():
    own = jnp.where(lax.axis_index("c") == lax.axis_index("xl"), 3, 0)
    left = jnp.where(lax.axis_index("xl") == 0, 3, 0)
    return [
        (pl.ds(lat, 3), pl.ds(lon, 6))
        for lat, lon in ((own, 6), (left, 0), (3 - own, 6), (3 - left, 0))
    ]


def pack_kernel(t_ref, g_ref, o0, o1, o2, o3, sems):
    copies = []
    for q, (out, (lat, lon)) in enumerate(zip((o0, o1, o2, o3), quadrants())):
        for i, field in enumerate((t_ref, g_ref)):
            copies.append(pltpu.make_async_copy(field.at[lat, lon], out.at[i], sems.at[q, i]))
    for copy in copies:
        copy.start()
    for copy in copies:
        copy.wait()


def unpack_kernel(p0, p1, p2, p3, mixed_ref, token_ref, sems):
    copies = []
    for q, (piece, (lat, lon)) in enumerate(zip((p0, p1, p2, p3), quadrants())):
        for i, field in enumerate((mixed_ref, token_ref)):
            copies.append(pltpu.make_async_copy(piece.at[i], field.at[lat, lon], sems.at[q, i]))
    for copy in copies:
        copy.start()
    for copy in copies:
        copy.wait()


def stage_kernel(w_ref, held_ref, turned_ref, order_ref):
    held_ref[...] = w_ref[...]
    order_ref[...] = order_matrix(0)
    turned_ref[...] = w_ref[3 * FEAT :, :].T


def order_matrix(window_axis):
    shape = (2 * WIN, 2 * WIN)
    row = lax.broadcasted_iota(jnp.int32, shape, window_axis)
    col = lax.broadcasted_iota(jnp.int32, shape, 1 - window_axis)
    outer = row >= WIN
    j = jnp.where(outer, row - WIN, row)
    level = j & 1
    source = 4 * (j >> 1) + jnp.where(outer, 3 * level, 1 + level)
    return (source == col).astype(f32).astype(bf16)


def put_rows(core, block, part, kept_ref, sent_ref):
    for h in range(0, HEADS, 2):
        for xl in range(2):
            for zl in range(2):
                two = []
                for c in range(2):
                    at = h * HEAD + zl * 32 + xl * 16 + c * 8
                    pair = [block[at : at + 8], block[at + HEAD : at + HEAD + 8]]
                    two.append(jnp.concatenate(pair, axis=0).astype(bf16))
                at = (part * 2 + h // 4) * 128 + xl * 64 + zl * 32 + (h % 4) * 8
                kept_ref[at : at + 16, :] = jnp.where(core == 0, two[0], two[1])
                sent_ref[at : at + 16, :] = jnp.where(core == 0, two[1], two[0])


def main_kernel(
    p2, p3, p1, p0, w_ref, wot_ref, order_ref,
    x_ref, g_ref, dqt_ref, dkt_ref, dvt_ref, ctxt_ref, kept_ref, sent_ref,
    rows_ref, s_ref, dp_ref, pb_ref, ds_ref,
):
    core = lax.axis_index("c")
    last = lax.axis_size(LAT) - 1
    upper = core == lax.axis_index("xl")
    seam = lax.axis_index("xh") * 4 + lax.axis_index("y") == jnp.where(upper, last, 0)
    order = order_ref[...]
    fields = []
    for i, ref in enumerate((x_ref, g_ref)):
        for q, piece in enumerate((p0, p1, p2, p3)):
            at = q * (WIN // 2)
            rows_ref[i, at : at + WIN // 2, :] = piece[i].astype(f32).reshape(WIN // 2, FEAT)
        field = nn(order, rows_ref[i].astype(bf16))
        fields.append(field)
        ref[...] = field.astype(bf16)
    normed = normalize(fields[0])[0].astype(bf16)
    grad = fields[1].astype(bf16)
    kvn = nt(normed, w_ref[FEAT : 3 * FEAT, :]).astype(bf16)
    key = lax.broadcasted_iota(jnp.int32, (WIN, WIN), 0)
    query = lax.broadcasted_iota(jnp.int32, (WIN, WIN), 1)
    apart = seam & ((key >= 72) != (query >= 72))
    levels = (key & 1) != (query & 1)
    zero = jnp.zeros((HEAD, WIN), bf16)
    halves = []
    for w in range(2):
        nw = normed[w * WIN : (w + 1) * WIN]
        qkvt = nt(w_ref[: 3 * FEAT, :], nw).astype(bf16)
        cgt = nt(wot_ref[...], grad[w * WIN : (w + 1) * WIN]).astype(bf16)
        qt, kt, vt = qkvt[:FEAT], qkvt[FEAT : 2 * FEAT], qkvt[2 * FEAT :]
        scaled_q = (qt.astype(f32) * 0.125).astype(bf16)
        scaled_c = (cgt.astype(f32) * 0.125).astype(bf16)
        halves.append((nw, qt, kt, vt, cgt, scaled_q, scaled_c))

    def scores(w, h):
        rows = slice(w * WIN, (w + 1) * WIN)
        pair = slice((h // 2) * 128, (h // 2) * 128 + 128)
        value = slice(FEAT + (h // 2) * 128, FEAT + (h // 2) * 128 + 128)
        mine = slice(h * HEAD, h * HEAD + HEAD)
        scaled_q, scaled_c = halves[w][5:]

        def padded(half):
            return jnp.concatenate([half, zero] if h % 2 == 0 else [zero, half], axis=0)

        s_ref[w, h] = nn(kvn[rows, pair], padded(scaled_q[mine]))
        dp_ref[w, h] = nn(kvn[rows, value], padded(scaled_c[mine]))

    def softmax(w, h):
        hidden = apart if w == 0 else apart | levels
        s = jnp.where(hidden, masked_score, s_ref[w, h] * LOG2E)
        e = jnp.exp2(s - jnp.max(s, axis=0, keepdims=True))
        p = e * (1.0 / jnp.sum(e, axis=0, keepdims=True))
        dp = dp_ref[w, h]
        pb_ref[w, h] = p.astype(bf16)
        ds_ref[w, h] = (p * (dp - jnp.sum(dp * p, axis=0, keepdims=True))).astype(bf16)

    def products(w, h):
        qt, kt, vt, cgt = halves[w][1:5]
        mine = slice(h * HEAD, h * HEAD + HEAD)
        pb = pb_ref[w, h]
        ds = ds_ref[w, h]
        ctxt_ref[w, mine, :] = nn(vt[mine], pb).astype(bf16)
        dvt_ref[w, mine, :] = nt(cgt[mine], pb).astype(bf16)
        dqt_ref[w, mine, :] = nn(kt[mine], ds).astype(bf16)
        dkt_ref[w, mine, :] = nt(qt[mine], ds).astype(bf16)

    for h in range(HEADS):
        scores(0, h)
    for h in range(HEADS):
        scores(1, h)
        softmax(0, h)
    for h in range(HEADS):
        products(0, h)
        softmax(1, h)
    for h in range(HEADS):
        products(1, h)
    for part, ref in enumerate((dqt_ref, dkt_ref, dvt_ref)):
        block = nn(ref[0], halves[0][0]) + nn(ref[1], halves[1][0])
        put_rows(core, block, part, kept_ref, sent_ref)
    block = nt(grad[:WIN].T, ctxt_ref[0]) + nt(grad[WIN:].T, ctxt_ref[1])
    put_rows(core, block, 3, kept_ref, sent_ref)


def back_kernel(
    x_ref, g_ref, w_ref, dqt_ref, dkt_ref, dvt_ref, ctxt_ref, o0, o1, o2, o3, rows_ref, win_ref
):
    for w in range(2):
        rows = slice(w * WIN, (w + 1) * WIN)
        x = x_ref[rows, :].astype(f32)
        normed_exact, inverse = normalize(x)
        win_ref[0, rows, :] = (x + nt(ctxt_ref[w].T, w_ref[3 * FEAT :, :])).astype(bf16)
        normed_grad = (
            nn(dqt_ref[w].T, w_ref[:FEAT, :])
            + nn(dkt_ref[w].T, w_ref[FEAT : 2 * FEAT, :])
            + nn(dvt_ref[w].T, w_ref[2 * FEAT : 3 * FEAT, :])
        )
        correction = (
            normed_grad
            - jnp.mean(normed_grad, axis=-1, keepdims=True)
            - normed_exact * jnp.mean(normed_grad * normed_exact, axis=-1, keepdims=True)
        )
        win_ref[1, rows, :] = (g_ref[rows, :].astype(f32) + inverse * correction).astype(bf16)
    order = order_matrix(1)
    for i in range(2):
        rows_ref[...] = nn(order, win_ref[i])
        for q, piece in enumerate((o0, o1, o2, o3)):
            for a in range(3):
                for b in range(6):
                    at = ((q * 3 + a) * 6 + b) * 4
                    piece[i, a, b] = rows_ref[at : at + 4, :].astype(bf16)


def shift(piece, lat, lon, back):
    n_lat, n_lon = lax.axis_size(LAT), lax.axis_size(LON)
    pairs = []
    for i in range(n_lat):
        for j in range(n_lon):
            from_lat = (i + (lat if j % 4 in (0, 3) else -lat)) % n_lat
            owner = from_lat * n_lon + (j + lon) % n_lon
            pairs.append((i * n_lon + j, owner) if back else (owner, i * n_lon + j))
    return lax.ppermute(piece, ALL, pairs)


def body(tokens, weights, out_grad):
    quads = [(QUAD, bf16)] * 4
    sems = [pltpu.SemaphoreType.DMA((4, 2))]
    moves = ((0, 0), (0, 1), (1, 0), (1, 1))
    sources = [
        pltpu.with_memory_space_constraint(a.transpose(1, 2, 0, 3), pltpu.HBM)
        for a in (tokens, out_grad)
    ]
    parts = list(call(pack_kernel, quads, sems, 4, sources, [HBM] * 2))
    for q in (2, 3, 1):
        parts[q] = shift(parts[q], *moves[q], False)
    wide = ((4 * FEAT, FEAT), bf16)
    square = ((FEAT, FEAT), bf16)
    turn = ((2 * WIN, 2 * WIN), bf16)
    held, turned, order = call(stage_kernel, [wide, square, turn], [], 8, (weights,))
    rows = ((2 * WIN, FEAT), bf16)
    square = ((2, FEAT, WIN), bf16)
    half = ((2 * FEAT, FEAT), bf16)

    def tiles(kind):
        return pltpu.VMEM((2, HEADS, WIN, WIN), kind)

    x, grad, dqt, dkt, dvt, ctxt, kept, sent = call(
        main_kernel,
        [rows] * 2 + [square] * 4 + [half] * 2,
        [pltpu.VMEM((2, 2 * WIN, FEAT), f32)] + [tiles(f32)] * 2 + [tiles(bf16)] * 2,
        20,
        (parts[2], parts[3], parts[1], parts[0], held, turned, order),
    )
    got = lax.ppermute(sent, "c", [(0, 1), (1, 0)])
    backs = call(
        back_kernel,
        quads,
        [pltpu.VMEM((2 * WIN, FEAT), f32), pltpu.VMEM((2, 2 * WIN, FEAT), bf16)],
        12,
        (x, grad, held, dqt, dkt, dvt, ctxt),
    )
    got, backs = lax.optimization_barrier((got, list(backs)))
    total = (kept.astype(f32) + got.astype(f32)).astype(bf16).reshape(32, 32, FEAT)
    total = lax.all_to_all(total, ("xh", "y", "xl", "zl"), 0, 0, tiled=True)
    for q in (2, 3, 1):
        backs[q] = shift(backs[q], *moves[q], True)
    total = jnp.sum(total.astype(f32), axis=0)
    total = total.reshape(4, 8, FEAT)
    at = lax.axis_index("zh")
    chunks = [lax.dynamic_index_in_dim(total, (at + d) % 4, 0, keepdims=False) for d in range(4)]
    for d in (2, 1, 3):
        pairs = [(i, (i + d) % 4) for i in range(4)]
        chunks[d] = lax.ppermute(chunks[d], "zh", pairs)
    field = ((6, 12, 4, FEAT), bf16)
    results = call(unpack_kernel, [field] * 2, sems, 4, backs, [ANY] * 4, HBM)
    chunks, results = lax.optimization_barrier((chunks, results))
    weight_grads = chunks[0] + chunks[2] + (chunks[1] + chunks[3])
    mixed, token_grads = (r.transpose(2, 0, 1, 3) for r in results)
    return mixed, token_grads, weight_grads


def solution(mesh):
    fine = Mesh(mesh.devices.reshape(2, 4, 4, 2, 2, 2), ALL)
    spread = P(None, LAT, LON, None)
    return jax.shard_map(
        body,
        mesh=fine,
        in_specs=(spread, P(), spread),
        out_specs=(spread, spread, P(ALL, None)),
        check_vma=False,
    )
```

```python
import jax
import jax.numpy as jnp
from jax import lax
from jax.experimental import pallas as pl
from jax.experimental.pallas import tpu as pltpu
from jax.sharding import Mesh, PartitionSpec as P

HEADS = 8
FEAT = 512
HEAD = 64
WIN = 144
epsilon = 1e-05
masked_score = -1e30
LAT = ("xh", "y")
LON = ("zh", "zl", "xl", "c")
ALL = LAT + LON
VMEM = pl.BlockSpec(memory_space=pltpu.VMEM)
HBM = pl.BlockSpec(memory_space=pltpu.HBM)
ANY = pl.BlockSpec(memory_space=pl.ANY)
LOG2E = 1.4426950408889634
f32 = jnp.float32
bf16 = jnp.bfloat16


def nn(a, b):
    return lax.dot_general(a, b, (((1,), (0,)), ((), ())), preferred_element_type=f32)


def nt(a, b):
    return lax.dot_general(a, b, (((1,), (1,)), ((), ())), preferred_element_type=f32)


def call(kernel, outs, scratch, mib, args, kinds=None, out_kind=VMEM):
    return pl.pallas_call(
        kernel,
        out_shape=[jax.ShapeDtypeStruct(s, d) for s, d in outs],
        in_specs=[VMEM] * len(args) if kinds is None else kinds,
        out_specs=[out_kind] * len(outs),
        scratch_shapes=scratch,
        compiler_params=pltpu.CompilerParams(vmem_limit_bytes=mib * 2**20),
    )(*args)


def normalize(x):
    mean = jnp.mean(x, axis=-1, keepdims=True)
    centred = x - mean
    inverse = lax.rsqrt(jnp.mean(centred * centred, axis=-1, keepdims=True) + epsilon)
    return centred * inverse, inverse


QUAD = (2, 3, 6, 4, FEAT)


def quadrants():
    own = jnp.where(lax.axis_index("c") == lax.axis_index("xl"), 3, 0)
    left = jnp.where(lax.axis_index("xl") == 0, 3, 0)
    return [
        (pl.ds(lat, 3), pl.ds(lon, 6))
        for lat, lon in ((own, 6), (left, 0), (3 - own, 6), (3 - left, 0))
    ]


def pack_kernel(t_ref, g_ref, o0, o1, o2, o3, sems):
    copies = []
    for q, (out, (lat, lon)) in enumerate(zip((o0, o1, o2, o3), quadrants())):
        for i, field in enumerate((t_ref, g_ref)):
            copies.append(pltpu.make_async_copy(field.at[lat, lon], out.at[i], sems.at[q, i]))
    for copy in copies:
        copy.start()
    for copy in copies:
        copy.wait()


def unpack_kernel(p0, p1, p2, p3, mixed_ref, token_ref, sems):
    copies = []
    for q, (piece, (lat, lon)) in enumerate(zip((p0, p1, p2, p3), quadrants())):
        for i, field in enumerate((mixed_ref, token_ref)):
            copies.append(pltpu.make_async_copy(piece.at[i], field.at[lat, lon], sems.at[q, i]))
    for copy in copies:
        copy.start()
    for copy in copies:
        copy.wait()


def stage_kernel(w_ref, held_ref, turned_ref, order_ref):
    held_ref[...] = w_ref[...]
    order_ref[...] = order_matrix(0)
    turned_ref[...] = w_ref[3 * FEAT :, :].T


def order_matrix(window_axis):
    shape = (2 * WIN, 2 * WIN)
    row = lax.broadcasted_iota(jnp.int32, shape, window_axis)
    col = lax.broadcasted_iota(jnp.int32, shape, 1 - window_axis)
    outer = row >= WIN
    j = jnp.where(outer, row - WIN, row)
    level = j & 1
    source = 4 * (j >> 1) + jnp.where(outer, 3 * level, 1 + level)
    return (source == col).astype(f32).astype(bf16)


def put_rows(core, block, part, kept_ref, sent_ref):
    for h in range(0, HEADS, 2):
        for xl in range(2):
            for zl in range(2):
                two = []
                for c in range(2):
                    at = h * HEAD + zl * 32 + xl * 16 + c * 8
                    pair = [block[at : at + 8], block[at + HEAD : at + HEAD + 8]]
                    two.append(jnp.concatenate(pair, axis=0))
                y = (part % 2) * 2 + h // 4
                at = zl * 512 + xl * 256 + y * 64 + (part // 2) * 32 + (h % 4) * 8
                kept_ref[at : at + 16, :] = jnp.where(core == 0, two[0], two[1]).astype(bf16)
                sent_ref[at : at + 16, :] = jnp.where(core == 0, two[1], two[0]).astype(bf16)


def main_kernel(
    p2, p3, p1, p0, w_ref, wot_ref, order_ref,
    x_ref, g_ref, dqt_ref, dkt_ref, dvt_ref, ctxt_ref, kept_ref, sent_ref,
    rows_ref, s_ref, dp_ref, pb_ref, ds_ref,
):
    core = lax.axis_index("c")
    last = lax.axis_size(LAT) - 1
    upper = core == lax.axis_index("xl")
    seam = lax.axis_index("xh") * 4 + lax.axis_index("y") == jnp.where(upper, last, 0)
    order = order_ref[...]
    fields = []
    for i, ref in enumerate((x_ref, g_ref)):
        for q, piece in enumerate((p0, p1, p2, p3)):
            for a in range(3):
                for b in range(6):
                    at = ((q * 3 + a) * 6 + b) * 4
                    rows_ref[i, at : at + 4, :] = piece[i, a, b].astype(f32)
        field = nn(order, rows_ref[i].astype(bf16))
        fields.append(field)
        ref[...] = field.astype(bf16)
    normed = normalize(fields[0])[0].astype(bf16)
    grad = fields[1].astype(bf16)
    kvn = nt(normed, w_ref[FEAT : 3 * FEAT, :]).astype(bf16)
    key = lax.broadcasted_iota(jnp.int32, (WIN, WIN), 0)
    query = lax.broadcasted_iota(jnp.int32, (WIN, WIN), 1)
    apart = seam & ((key >= 72) != (query >= 72))
    levels = (key & 1) != (query & 1)
    zero = jnp.zeros((HEAD, WIN), bf16)
    halves = []
    for w in range(2):
        nw = normed[w * WIN : (w + 1) * WIN]
        qkvt = nt(w_ref[: 3 * FEAT, :], nw).astype(bf16)
        cgt = nt(wot_ref[...], grad[w * WIN : (w + 1) * WIN]).astype(bf16)
        qt, kt, vt = qkvt[:FEAT], qkvt[FEAT : 2 * FEAT], qkvt[2 * FEAT :]
        scaled_q = (qt.astype(f32) * 0.125).astype(bf16)
        scaled_c = (cgt.astype(f32) * 0.125).astype(bf16)
        halves.append((nw, qt, kt, vt, cgt, scaled_q, scaled_c))

    def scores(w, h):
        rows = slice(w * WIN, (w + 1) * WIN)
        pair = slice((h // 2) * 128, (h // 2) * 128 + 128)
        value = slice(FEAT + (h // 2) * 128, FEAT + (h // 2) * 128 + 128)
        mine = slice(h * HEAD, h * HEAD + HEAD)
        scaled_q, scaled_c = halves[w][5:]

        def padded(half):
            return jnp.concatenate([half, zero] if h % 2 == 0 else [zero, half], axis=0)

        s_ref[w, h] = nn(kvn[rows, pair], padded(scaled_q[mine]))
        dp_ref[w, h] = nn(kvn[rows, value], padded(scaled_c[mine]))

    def softmax(w, h):
        hidden = apart if w == 0 else apart | levels
        s = jnp.where(hidden, masked_score, s_ref[w, h] * LOG2E)
        e = jnp.exp2(s - jnp.max(s, axis=0, keepdims=True))
        p = e * (1.0 / jnp.sum(e, axis=0, keepdims=True))
        dp = dp_ref[w, h]
        pb_ref[w, h] = p.astype(bf16)
        ds_ref[w, h] = (p * (dp - jnp.sum(dp * p, axis=0, keepdims=True))).astype(bf16)

    def products(w, h):
        qt, kt, vt, cgt = halves[w][1:5]
        mine = slice(h * HEAD, h * HEAD + HEAD)
        pb = pb_ref[w, h]
        ds = ds_ref[w, h]
        ctxt_ref[w, mine, :] = nn(vt[mine], pb).astype(bf16)
        dvt_ref[w, mine, :] = nt(cgt[mine], pb).astype(bf16)
        dqt_ref[w, mine, :] = nn(kt[mine], ds).astype(bf16)
        dkt_ref[w, mine, :] = nt(qt[mine], ds).astype(bf16)

    for h in range(HEADS):
        scores(0, h)
    for h in range(HEADS):
        scores(1, h)
        softmax(0, h)
    for h in range(HEADS):
        products(0, h)
        softmax(1, h)
    for h in range(HEADS):
        products(1, h)
    for part, ref in enumerate((dqt_ref, dkt_ref, dvt_ref)):
        block = nn(ref[0], halves[0][0]) + nn(ref[1], halves[1][0])
        put_rows(core, block, part, kept_ref, sent_ref)
    block = nt(grad[:WIN].T, ctxt_ref[0]) + nt(grad[WIN:].T, ctxt_ref[1])
    put_rows(core, block, 3, kept_ref, sent_ref)


def back_kernel(
    x_ref, g_ref, w_ref, dqt_ref, dkt_ref, dvt_ref, ctxt_ref, o0, o1, o2, o3, rows_ref, win_ref
):
    for w in range(2):
        rows = slice(w * WIN, (w + 1) * WIN)
        x = x_ref[rows, :].astype(f32)
        normed_exact, inverse = normalize(x)
        win_ref[0, rows, :] = (x + nt(ctxt_ref[w].T, w_ref[3 * FEAT :, :])).astype(bf16)
        normed_grad = (
            nn(dqt_ref[w].T, w_ref[:FEAT, :])
            + nn(dkt_ref[w].T, w_ref[FEAT : 2 * FEAT, :])
            + nn(dvt_ref[w].T, w_ref[2 * FEAT : 3 * FEAT, :])
        )
        correction = (
            normed_grad
            - jnp.mean(normed_grad, axis=-1, keepdims=True)
            - normed_exact * jnp.mean(normed_grad * normed_exact, axis=-1, keepdims=True)
        )
        win_ref[1, rows, :] = (g_ref[rows, :].astype(f32) + inverse * correction).astype(bf16)
    order = order_matrix(1)
    for i in range(2):
        rows_ref[...] = nn(order, win_ref[i])
        for q, piece in enumerate((o0, o1, o2, o3)):
            for a in range(3):
                for b in range(6):
                    at = ((q * 3 + a) * 6 + b) * 4
                    piece[i, a, b] = rows_ref[at : at + 4, :].astype(bf16)


def shift(piece, lat, lon, back):
    n_lat, n_lon = lax.axis_size(LAT), lax.axis_size(LON)
    pairs = []
    for i in range(n_lat):
        for j in range(n_lon):
            from_lat = (i + (lat if j % 4 in (0, 3) else -lat)) % n_lat
            owner = from_lat * n_lon + (j + lon) % n_lon
            pairs.append((i * n_lon + j, owner) if back else (owner, i * n_lon + j))
    return lax.ppermute(piece, ALL, pairs)


def body(tokens, weights, out_grad):
    quads = [(QUAD, bf16)] * 4
    sems = [pltpu.SemaphoreType.DMA((4, 2))]
    moves = ((0, 0), (0, 1), (1, 0), (1, 1))
    sources = [
        pltpu.with_memory_space_constraint(a.transpose(1, 2, 0, 3), pltpu.HBM)
        for a in (tokens, out_grad)
    ]
    parts = list(call(pack_kernel, quads, sems, 4, sources, [HBM] * 2))
    for q in (2, 3, 1):
        parts[q] = shift(parts[q], *moves[q], False)
    wide = ((4 * FEAT, FEAT), bf16)
    square = ((FEAT, FEAT), bf16)
    turn = ((2 * WIN, 2 * WIN), bf16)
    held, turned, order = call(stage_kernel, [wide, square, turn], [], 8, (weights,))
    rows = ((2 * WIN, FEAT), bf16)
    square = ((2, FEAT, WIN), bf16)
    half = ((2 * FEAT, FEAT), bf16)

    def tiles(kind):
        return pltpu.VMEM((2, HEADS, WIN, WIN), kind)

    x, grad, dqt, dkt, dvt, ctxt, kept, sent = call(
        main_kernel,
        [rows] * 2 + [square] * 4 + [half] * 2,
        [pltpu.VMEM((2, 2 * WIN, FEAT), f32)] + [tiles(f32)] * 2 + [tiles(bf16)] * 2,
        20,
        (parts[2], parts[3], parts[1], parts[0], held, turned, order),
    )
    got = lax.ppermute(sent, "c", [(0, 1), (1, 0)])
    backs = call(
        back_kernel,
        quads,
        [pltpu.VMEM((2 * WIN, FEAT), f32), pltpu.VMEM((2, 2 * WIN, FEAT), bf16)],
        12,
        (x, grad, held, dqt, dkt, dvt, ctxt),
    )
    got, backs = lax.optimization_barrier((got, list(backs)))
    total = (kept.astype(f32) + got.astype(f32)).astype(bf16).reshape(32, 32, FEAT)
    total = lax.all_to_all(total, ("zl", "xl", "y", "xh"), 0, 0, tiled=True)
    for q in (2, 3, 1):
        backs[q] = shift(backs[q], *moves[q], True)
    total = jnp.sum(total.astype(f32), axis=0)
    total = total.reshape(4, 8, FEAT)
    at = lax.axis_index("zh")
    chunks = [lax.dynamic_index_in_dim(total, (at + d) % 4, 0, keepdims=False) for d in range(4)]
    for d in (2, 1, 3):
        pairs = [(i, (i + d) % 4) for i in range(4)]
        chunks[d] = lax.ppermute(chunks[d], "zh", pairs)
    field = ((6, 12, 4, FEAT), bf16)
    results = call(unpack_kernel, [field] * 2, sems, 4, backs, [ANY] * 4, HBM)
    chunks, results = lax.optimization_barrier((chunks, results))
    weight_grads = chunks[0] + chunks[2] + (chunks[1] + chunks[3])
    mixed, token_grads = (r.transpose(2, 0, 1, 3) for r in results)
    return mixed, token_grads, weight_grads


def solution(mesh):
    fine = Mesh(mesh.devices.reshape(2, 4, 4, 2, 2, 2), ALL)
    spread = P(None, LAT, LON, None)
    return jax.shard_map(
        body,
        mesh=fine,
        in_specs=(spread, P(), spread),
        out_specs=(spread, spread, P(ALL, None)),
        check_vma=False,
    )
```

```python
import jax
import jax.numpy as jnp
from jax import lax
from jax.experimental import pallas as pl
from jax.experimental.pallas import tpu as pltpu
from jax.sharding import Mesh, PartitionSpec as P

HEADS = 8
FEAT = 512
HEAD = 64
WIN = 144
epsilon = 1e-05
masked_score = -1e30
LAT = ("xh", "y")
LON = ("zh", "zl", "xl", "c")
ALL = LAT + LON
VMEM = pl.BlockSpec(memory_space=pltpu.VMEM)
HBM = pl.BlockSpec(memory_space=pltpu.HBM)
ANY = pl.BlockSpec(memory_space=pl.ANY)
LOG2E = 1.4426950408889634
f32 = jnp.float32
bf16 = jnp.bfloat16


def nn(a, b):
    return lax.dot_general(a, b, (((1,), (0,)), ((), ())), preferred_element_type=f32)


def nt(a, b):
    return lax.dot_general(a, b, (((1,), (1,)), ((), ())), preferred_element_type=f32)


def call(kernel, outs, scratch, mib, args, kinds=None, out_kind=VMEM):
    return pl.pallas_call(
        kernel,
        out_shape=[jax.ShapeDtypeStruct(s, d) for s, d in outs],
        in_specs=[VMEM] * len(args) if kinds is None else kinds,
        out_specs=[out_kind] * len(outs),
        scratch_shapes=scratch,
        compiler_params=pltpu.CompilerParams(vmem_limit_bytes=mib * 2**20),
    )(*args)


def normalize(x):
    mean = jnp.mean(x, axis=-1, keepdims=True)
    centred = x - mean
    inverse = lax.rsqrt(jnp.mean(centred * centred, axis=-1, keepdims=True) + epsilon)
    return centred * inverse, inverse


QUAD = (2, 3, 6, 4, FEAT)


def quadrants():
    own = jnp.where(lax.axis_index("c") == lax.axis_index("xl"), 3, 0)
    left = jnp.where(lax.axis_index("xl") == 0, 3, 0)
    return [
        (pl.ds(lat, 3), pl.ds(lon, 6))
        for lat, lon in ((own, 6), (left, 0), (3 - own, 6), (3 - left, 0))
    ]


def pack_kernel(t_ref, g_ref, o0, o1, o2, o3, sems):
    copies = []
    for q, (out, (lat, lon)) in enumerate(zip((o0, o1, o2, o3), quadrants())):
        for i, field in enumerate((t_ref, g_ref)):
            copies.append(pltpu.make_async_copy(field.at[lat, lon], out.at[i], sems.at[q, i]))
    for copy in copies:
        copy.start()
    for copy in copies:
        copy.wait()


def unpack_kernel(p0, p1, p2, p3, mixed_ref, token_ref, sems):
    copies = []
    for q, (piece, (lat, lon)) in enumerate(zip((p0, p1, p2, p3), quadrants())):
        for i, field in enumerate((mixed_ref, token_ref)):
            copies.append(pltpu.make_async_copy(piece.at[i], field.at[lat, lon], sems.at[q, i]))
    for copy in copies:
        copy.start()
    for copy in copies:
        copy.wait()


def stage_kernel(w_ref, held_ref, turned_ref, order_ref):
    held_ref[...] = w_ref[...]
    order_ref[...] = order_matrix(0)
    turned_ref[...] = w_ref[3 * FEAT :, :].T


def order_matrix(window_axis):
    shape = (2 * WIN, 2 * WIN)
    row = lax.broadcasted_iota(jnp.int32, shape, window_axis)
    col = lax.broadcasted_iota(jnp.int32, shape, 1 - window_axis)
    outer = row >= WIN
    j = jnp.where(outer, row - WIN, row)
    level = j & 1
    source = 4 * (j >> 1) + jnp.where(outer, 3 * level, 1 + level)
    return (source == col).astype(f32).astype(bf16)


def put_rows(core, block, part, kept_ref, sent_ref):
    for h in range(0, HEADS, 2):
        for xl in range(2):
            for zl in range(2):
                two = []
                for c in range(2):
                    at = h * HEAD + zl * 32 + xl * 16 + c * 8
                    pair = [block[at : at + 8], block[at + HEAD : at + HEAD + 8]]
                    two.append(jnp.concatenate(pair, axis=0))
                y = (part % 2) * 2 + h // 4
                at = zl * 512 + xl * 256 + y * 64 + (part // 2) * 32 + (h % 4) * 8
                kept_ref[at : at + 16, :] = jnp.where(core == 0, two[0], two[1]).astype(bf16)
                sent_ref[at : at + 16, :] = jnp.where(core == 0, two[1], two[0]).astype(bf16)


def main_kernel(
    p2, p3, p1, p0, w_ref, wot_ref, order_ref,
    x_ref, g_ref, dqt_ref, dkt_ref, dvt_ref, ctxt_ref, kept_ref, sent_ref,
    rows_ref, s_ref, dp_ref, pb_ref, ds_ref,
):
    core = lax.axis_index("c")
    last = lax.axis_size(LAT) - 1
    upper = core == lax.axis_index("xl")
    seam = lax.axis_index("xh") * 4 + lax.axis_index("y") == jnp.where(upper, last, 0)
    order = order_ref[...]
    fields = []
    for i, ref in enumerate((x_ref, g_ref)):
        for q, piece in enumerate((p0, p1, p2, p3)):
            for a in range(3):
                for b in range(6):
                    at = ((q * 3 + a) * 6 + b) * 4
                    rows_ref[i, at : at + 4, :] = piece[i, a, b].astype(f32)
        field = nn(order, rows_ref[i].astype(bf16))
        fields.append(field)
        ref[...] = field.astype(bf16)
    normed = normalize(fields[0])[0].astype(bf16)
    grad = fields[1].astype(bf16)
    kvn = nt(normed, w_ref[FEAT : 3 * FEAT, :]).astype(bf16)
    key = lax.broadcasted_iota(jnp.int32, (WIN, WIN), 0)
    query = lax.broadcasted_iota(jnp.int32, (WIN, WIN), 1)
    apart = seam & ((key >= 72) != (query >= 72))
    levels = (key & 1) != (query & 1)
    zero = jnp.zeros((HEAD, WIN), bf16)
    halves = []
    for w in range(2):
        nw = normed[w * WIN : (w + 1) * WIN]
        qkvt = nt(w_ref[: 3 * FEAT, :], nw).astype(bf16)
        cgt = nt(wot_ref[...], grad[w * WIN : (w + 1) * WIN]).astype(bf16)
        qt, kt, vt = qkvt[:FEAT], qkvt[FEAT : 2 * FEAT], qkvt[2 * FEAT :]
        scaled_q = (qt.astype(f32) * 0.125).astype(bf16)
        scaled_c = (cgt.astype(f32) * 0.125).astype(bf16)
        halves.append((nw, qt, kt, vt, cgt, scaled_q, scaled_c))

    def scores(w, h):
        rows = slice(w * WIN, (w + 1) * WIN)
        pair = slice((h // 2) * 128, (h // 2) * 128 + 128)
        value = slice(FEAT + (h // 2) * 128, FEAT + (h // 2) * 128 + 128)
        mine = slice(h * HEAD, h * HEAD + HEAD)
        scaled_q, scaled_c = halves[w][5:]

        def padded(half):
            return jnp.concatenate([half, zero] if h % 2 == 0 else [zero, half], axis=0)

        s_ref[w, h] = nn(kvn[rows, pair], padded(scaled_q[mine]))
        dp_ref[w, h] = nn(kvn[rows, value], padded(scaled_c[mine]))

    def softmax(w, h):
        hidden = apart if w == 0 else apart | levels
        s = jnp.where(hidden, masked_score, s_ref[w, h] * LOG2E)
        e = jnp.exp2(s - jnp.max(s, axis=0, keepdims=True))
        p = e * (1.0 / jnp.sum(e, axis=0, keepdims=True))
        dp = dp_ref[w, h]
        pb_ref[w, h] = p.astype(bf16)
        ds_ref[w, h] = (p * (dp - jnp.sum(dp * p, axis=0, keepdims=True))).astype(bf16)

    def products(w, h):
        qt, kt, vt, cgt = halves[w][1:5]
        mine = slice(h * HEAD, h * HEAD + HEAD)
        pb = pb_ref[w, h]
        ds = ds_ref[w, h]
        ctxt_ref[w, mine, :] = nn(vt[mine], pb).astype(bf16)
        dvt_ref[w, mine, :] = nt(cgt[mine], pb).astype(bf16)
        dqt_ref[w, mine, :] = nn(kt[mine], ds).astype(bf16)
        dkt_ref[w, mine, :] = nt(qt[mine], ds).astype(bf16)

    for h in range(HEADS):
        scores(0, h)
    for h in range(HEADS):
        scores(1, h)
        softmax(0, h)
    for h in range(HEADS):
        products(0, h)
        softmax(1, h)
    for h in range(HEADS):
        products(1, h)
    for part, ref in enumerate((dqt_ref, dkt_ref, dvt_ref)):
        block = nn(ref[0], halves[0][0]) + nn(ref[1], halves[1][0])
        put_rows(core, block, part, kept_ref, sent_ref)
    block = nt(grad[:WIN].T, ctxt_ref[0]) + nt(grad[WIN:].T, ctxt_ref[1])
    put_rows(core, block, 3, kept_ref, sent_ref)


def back_kernel(
    x_ref, g_ref, w_ref, dqt_ref, dkt_ref, dvt_ref, ctxt_ref, o0, o1, o2, o3, rows_ref, win_ref
):
    for w in range(2):
        rows = slice(w * WIN, (w + 1) * WIN)
        x = x_ref[rows, :].astype(f32)
        normed_exact, inverse = normalize(x)
        win_ref[0, rows, :] = (x + nt(ctxt_ref[w].T, w_ref[3 * FEAT :, :])).astype(bf16)
        normed_grad = (
            nn(dqt_ref[w].T, w_ref[:FEAT, :])
            + nn(dkt_ref[w].T, w_ref[FEAT : 2 * FEAT, :])
            + nn(dvt_ref[w].T, w_ref[2 * FEAT : 3 * FEAT, :])
        )
        correction = (
            normed_grad
            - jnp.mean(normed_grad, axis=-1, keepdims=True)
            - normed_exact * jnp.mean(normed_grad * normed_exact, axis=-1, keepdims=True)
        )
        win_ref[1, rows, :] = (g_ref[rows, :].astype(f32) + inverse * correction).astype(bf16)
    order = order_matrix(1)
    for i in range(2):
        rows_ref[...] = nn(order, win_ref[i])
        for q, piece in enumerate((o0, o1, o2, o3)):
            for a in range(3):
                for b in range(6):
                    at = ((q * 3 + a) * 6 + b) * 4
                    piece[i, a, b] = rows_ref[at : at + 4, :].astype(bf16)


def shift(piece, lat, lon, back):
    n_lat, n_lon = lax.axis_size(LAT), lax.axis_size(LON)
    pairs = []
    for i in range(n_lat):
        for j in range(n_lon):
            from_lat = (i + (lat if j % 4 in (0, 3) else -lat)) % n_lat
            owner = from_lat * n_lon + (j + lon) % n_lon
            pairs.append((i * n_lon + j, owner) if back else (owner, i * n_lon + j))
    return lax.ppermute(piece, ALL, pairs)


def body(tokens, weights, out_grad):
    quads = [(QUAD, bf16)] * 4
    sems = [pltpu.SemaphoreType.DMA((4, 2))]
    moves = ((0, 0), (0, 1), (1, 0), (1, 1))
    sources = [
        pltpu.with_memory_space_constraint(a.transpose(1, 2, 0, 3), pltpu.HBM)
        for a in (tokens, out_grad)
    ]
    parts = list(call(pack_kernel, quads, sems, 4, sources, [HBM] * 2))
    for q in (2, 3, 1):
        parts[q] = shift(parts[q], *moves[q], False)
    wide = ((4 * FEAT, FEAT), bf16)
    square = ((FEAT, FEAT), bf16)
    turn = ((2 * WIN, 2 * WIN), bf16)
    held, turned, order = call(stage_kernel, [wide, square, turn], [], 8, (weights,))
    rows = ((2 * WIN, FEAT), bf16)
    square = ((2, FEAT, WIN), bf16)
    half = ((2 * FEAT, FEAT), bf16)

    def tiles(kind):
        return pltpu.VMEM((2, HEADS, WIN, WIN), kind)

    x, grad, dqt, dkt, dvt, ctxt, kept, sent = call(
        main_kernel,
        [rows] * 2 + [square] * 4 + [half] * 2,
        [pltpu.VMEM((2, 2 * WIN, FEAT), f32)] + [tiles(f32)] * 2 + [tiles(bf16)] * 2,
        20,
        (parts[2], parts[3], parts[1], parts[0], held, turned, order),
    )
    got = lax.ppermute(sent, "c", [(0, 1), (1, 0)])
    backs = call(
        back_kernel,
        quads,
        [pltpu.VMEM((2 * WIN, FEAT), f32), pltpu.VMEM((2, 2 * WIN, FEAT), bf16)],
        12,
        (x, grad, held, dqt, dkt, dvt, ctxt),
    )
    got, backs = lax.optimization_barrier((got, list(backs)))
    total = (kept.astype(f32) + got.astype(f32)).astype(bf16).reshape(32, 32, FEAT)
    total = lax.all_to_all(total, ("zl", "xl", "y", "xh"), 0, 0, tiled=True)
    for q in (2, 3, 1):
        backs[q] = shift(backs[q], *moves[q], True)
    total = jnp.sum(total.astype(f32), axis=0)
    at = lax.axis_index("zh")

    def halves(rows, bit):
        rows = rows.reshape(2, 8 * bit, FEAT)
        mine = (at // bit) % 2
        stays = lax.dynamic_index_in_dim(rows, mine, 0, keepdims=False)
        gone = lax.dynamic_index_in_dim(rows, 1 - mine, 0, keepdims=False)
        return stays, lax.ppermute(gone, "zh", [(i, i ^ bit) for i in range(4)])

    stays, came = halves(total, 2)
    field = ((6, 12, 4, FEAT), bf16)
    results = call(unpack_kernel, [field] * 2, sems, 4, backs, [ANY] * 4, HBM)
    came, results = lax.optimization_barrier((came, results))
    stays, came = halves(stays + came, 1)
    weight_grads = stays + came
    mixed, token_grads = (r.transpose(2, 0, 1, 3) for r in results)
    return mixed, token_grads, weight_grads


def solution(mesh):
    fine = Mesh(mesh.devices.reshape(2, 4, 4, 2, 2, 2), ALL)
    spread = P(None, LAT, LON, None)
    return jax.shard_map(
        body,
        mesh=fine,
        in_specs=(spread, P(), spread),
        out_specs=(spread, spread, P(ALL, None)),
        check_vma=False,
    )
```
